128 devices in a mesh: grp: 8 (over x, core), dev: 16 (over y, z).
Axes of the slice: x: 4, y: 4, z: 4, core: 2. Of those that a mesh axis runs over, the one named last changes fastest.
Arguments:
- q_nope: bfloat16 [1024, 8192], P('grp', 'dev'), may hold values from -6 to 6
- q_rope: bfloat16 [1024, 4096], P('grp', 'dev'), may hold values from -60 to 60
- w_absorb_k: bfloat16 [64, 128, 512], P('dev'), may hold values from -0.5 to 0.5
- latent_cache: bfloat16 [1024, 512, 512], P(('grp', 'dev')), may hold values from -6 to 6
- rope_keys: bfloat16 [1024, 64, 512], P(('grp', 'dev')), may hold values from -9 to 9
- cache_lengths: int32 [1024], P(('grp', 'dev')), may hold values from 2 to 512, as said below
- w_absorb_v: bfloat16 [64, 512, 128], P('dev'), may hold values from -0.25 to 0.25
- w_out: bfloat16 [8192, 7168], P('dev'), may hold values from -0.0625 to 0.0625
- norm_gain: float32 [7168], replicated, may hold values from 0.5 to 1.5
- routes: int32 [1024, 4], P(('grp', 'dev')), may hold values from 0 to 15, all different within a row; in each aligned block of 8 rows (0 to 7, 8 to 15, ...) at most 4 rows name the same one
- expert_probs: float32 [1024, 4], P(('grp', 'dev')), may hold values from 0.05 to 1
- group_probs: float32 [1024, 8], P(('grp', 'dev')), may hold values from 0.1 to 1
- w_gate: bfloat16 [128, 7168, 256], P(('grp', 'dev')), may hold values from -0.0625 to 0.0625
- w_up: bfloat16 [128, 7168, 256], P(('grp', 'dev')), may hold values from -0.0625 to 0.0625
- w_down: bfloat16 [128, 256, 7168], P(('grp', 'dev')), may hold values from -0.125 to 0.125
Outputs:
- moe_out: bfloat16 [1024, 7168], P(('grp', 'dev'))
The draws below stay inside these ranges and needn't reach their ends.
Inputs may be any that keep to these rules, and one draw needn't show every extreme that they name: `routes`: in each aligned block of 8 rows (the rows of one device) no expert is named by more than 4 rows, a bound that some block reaches; a row names 4 different experts. A request's live cache positions are the first cache_lengths of its 512; some request holds all 512.
All inputs are finite; a program needn't handle non-finite values.
Results may differ from the reference program's by a relative error of at most 0.035.
Values may be sent and summed in bfloat16 or wider, within the bound.
No kernel may reach another device: no remote copies, remote signals or barrier semaphores. Data moves between devices by JAX's collectives and lax.ppermute only.
A program may use at most 128 MiB of HBM per device.

```python
import math
import jax
import jax.numpy as jnp
import numpy as np
from jax import lax

D = 7168
NOPE = 128
ROPE = 64
LATENT = 512
VHEAD = 128
MOE_HID = 2048
EXP_GRP = 2
TOPK = 4
R_DEV = 8
CAP_LEN = 512
HEADS = 64
SHARDS = 8
HID_DEV = 256
EXPERTS = 16
CAP = 4
TOKENS = 1024
N_GRP = 8


def draw_q_rope(key, part):
    key = jax.random.fold_in(key, 11)
    drawn = jnp.clip(jax.random.normal(key, (TOKENS, HEADS, ROPE), jnp.float32), -4.0, 4.0)
    return drawn.reshape(TOKENS, HEADS * ROPE).astype(jnp.bfloat16)


def draw_rope_keys(key, part):
    key = jax.random.fold_in(key, 12)
    first = jax.random.fold_in(key, 0)
    drawn = jnp.clip(jax.random.normal(first, (TOKENS, ROPE, CAP_LEN), jnp.float32), -4.0, 4.0)
    return drawn.astype(jnp.bfloat16)


def draw_cache_lengths(key, part):
    key = jax.random.fold_in(key, 13)
    first, second, third = jax.random.split(key, 3)
    lead = jax.random.randint(first, (TOKENS,), 1, CAP_LEN + 1)
    trail = jax.random.randint(second, (TOKENS,), 1, CAP_LEN + 1)
    lengths = jnp.maximum(lead * trail // CAP_LEN, 2)
    longest = jax.random.randint(third, (), 0, TOKENS)
    return jnp.where(jnp.arange(TOKENS) == longest, CAP_LEN, lengths).astype(jnp.int32)


def shard_levels(own_key, dims, cuts, low, top_value):
    gain, own = 1.0, jax.random.fold_in(own_key, 6)
    for dim, shards_of in cuts:
        steps = jnp.exp(jax.random.uniform(jax.random.fold_in(own, dim), (shards_of,), jnp.float32, low / len(cuts), top_value / len(cuts)))
        gain = gain * jnp.repeat(steps, dims[dim] // shards_of).reshape([-1 if axis == dim else 1 for axis in range(len(dims))])
    return gain


def assign_block(stream_key, own, number, rows, number_of, top, bound, skew):
    sequence = jax.random.permutation(stream_key, number_of)
    crowded, usual = shares(number_of, rows * top, bound, skew, True), shares(number_of, rows * top, bound, skew, False)
    places = jnp.arange(number_of)

    def named(sizes, rotation):
        used = int((sizes > 0).sum())
        fixed = max(1, used // 4)
        moved = fixed + (places - fixed + rotation * (used - fixed)) % max(1, number_of - fixed)
        return jnp.zeros((number_of,), jnp.int32).at[sequence[jnp.where(places < fixed, places, moved)]].set(jnp.asarray(sizes, jnp.int32))

    sizes = jnp.where(number % 4 == 0, named(crowded, number // 4), named(usual, number - number // 4 - 1))
    mixed = jax.random.permutation(jax.random.fold_in(own, 3), number_of)
    giver, receiver = mixed[0:number_of // 2 * 2:2], mixed[1:number_of // 2 * 2:2]
    margin = jnp.minimum(sizes[giver] - 1, bound - sizes[receiver]) // 2
    margin = jnp.where((giver == sequence[0]) | (receiver == sequence[0]) | (sizes[receiver] == 0), 0, jnp.maximum(margin, 0))
    moved = jax.random.randint(jax.random.fold_in(own, 4), (number_of // 2,), 0, 1 << 20) % (margin + 1)
    sizes = sizes.at[giver].add(-moved).at[receiver].add(moved)
    items = jnp.searchsorted(jnp.cumsum(sizes), jnp.arange(rows * top), side="right").astype(jnp.int32)
    table = items.reshape(top, rows).T
    table = table[jax.random.permutation(jax.random.fold_in(own, 1), rows)]
    rotation = jax.random.randint(jax.random.fold_in(own, 2), (rows, 1), 0, top)
    return jnp.take_along_axis(table, (jnp.arange(top)[None, :] + rotation) % top, axis=1)


def shares(number_of, total, bound, slope, full):
    loads = [(1 << 20) // math.isqrt(standing ** slope) + 1 for standing in range(1, number_of + 1)]
    largest = bound if full else min(bound, max(-(-total // number_of), total * loads[0] // sum(loads)))
    least = 1 if total - largest >= number_of - 1 else 0
    given, surplus = [largest] + [least] * (number_of - 1), total - largest - least * (number_of - 1)
    while surplus > 0:
        free = [i for i in range(1, number_of) if given[i] < largest] or [i for i in range(1, number_of) if given[i] < bound]
        pool, left = sum([loads[i] for i in free]), surplus
        for i in free:
            more = min(bound - given[i], max(1, left * loads[i] // pool), surplus)
            given[i] = given[i] + more
            surplus = surplus - more
    return np.array(given)


def gaussian(rng, dims, scale, most, cuts=(), kind=jnp.bfloat16):
    factor_of = shard_levels(rng, dims, cuts, -0.22, 0.18) if cuts else 1.0
    array = jax.random.normal(rng, dims, jnp.float32) * scale * factor_of
    return jnp.minimum(jnp.maximum(array, -most), most).astype(kind)


def setup_inputs(seed: int = 0) -> dict:
    key_of = jax.random.split(jax.random.key(seed), 16)
    q_nope = gaussian(key_of[0], (TOKENS, HEADS * NOPE), 1.0, 6.0, ((0, 8), (1, 16)))
    q_rope = draw_q_rope(jax.random.fold_in(key_of[15], 71), 0)
    w_absorb_k = gaussian(key_of[2], (HEADS, NOPE, LATENT), NOPE ** -0.5, 0.5, ((0, 16),))
    latent_cache = gaussian(key_of[3], (TOKENS, CAP_LEN, LATENT), 1.0, 6.0, ((0, 128),))
    rope_keys = draw_rope_keys(jax.random.fold_in(key_of[15], 71), 0)
    cache_lengths = draw_cache_lengths(jax.random.fold_in(key_of[15], 71), 0)
    w_absorb_v = gaussian(key_of[6], (HEADS, LATENT, VHEAD), LATENT ** -0.5, 0.25, ((0, 16),))
    w_out = gaussian(key_of[7], (HEADS * VHEAD, D), (HEADS * VHEAD) ** -0.5, 0.0625, ((0, 16),))
    norm_gain = jnp.clip(1.0 + 0.1 * jax.random.normal(key_of[8], (D,), jnp.float32), 0.5, 1.5)
    routes_keys = jax.random.split(jax.random.fold_in(key_of[9], 1), TOKENS // R_DEV)
    routes_turns = jax.random.permutation(jax.random.fold_in(key_of[9], 3), TOKENS // R_DEV)
    routes = jax.vmap(lambda own, number: assign_block(jax.random.fold_in(key_of[9], 2), own, number, R_DEV, EXPERTS, TOPK, CAP, 2))(routes_keys, routes_turns).reshape((TOKENS, TOPK))
    expert_probs = jnp.clip(0.05 + 0.95 * jax.random.uniform(key_of[10], (TOKENS, TOPK), jnp.float32) ** shard_levels(key_of[10], (TOKENS, TOPK), ((0, 128),), -0.2, 0.2), 0.05, 1.0)
    group_probs = jnp.clip(0.1 + 0.9 * jax.random.uniform(key_of[11], (TOKENS, N_GRP), jnp.float32) ** shard_levels(key_of[11], (TOKENS, N_GRP), ((0, 128),), -0.2, 0.2), 0.1, 1.0)
    w_gate = gaussian(key_of[12], (EXPERTS * SHARDS, D, HID_DEV), D ** -0.5, 0.0625, ((0, 128),))
    w_up = gaussian(key_of[13], (EXPERTS * SHARDS, D, HID_DEV), D ** -0.5, 0.0625, ((0, 128),))
    w_down = gaussian(key_of[14], (EXPERTS * SHARDS, HID_DEV, D), MOE_HID ** -0.5, 0.125, ((0, 128),))
    return dict(q_nope=q_nope, q_rope=q_rope, w_absorb_k=w_absorb_k, latent_cache=latent_cache, rope_keys=rope_keys, cache_lengths=cache_lengths, w_absorb_v=w_absorb_v, w_out=w_out, norm_gain=norm_gain, routes=routes, expert_probs=expert_probs, group_probs=group_probs, w_gate=w_gate, w_up=w_up, w_down=w_down)


def attend_block(operands):
    query_latent, query_rope, cache_block, key_block, length_block = operands
    softmax_scale = float(NOPE + ROPE) ** (-0.5)
    scores = jnp.einsum('rhc,rlc->rhl', query_latent.astype(jnp.float32), cache_block.astype(jnp.float32))
    scores = scores + jnp.einsum('rhp,rpl->rhl', query_rope.astype(jnp.float32), key_block.astype(jnp.float32))
    scores = scores * softmax_scale
    visible = jnp.arange(CAP_LEN, dtype=jnp.int32)[None, None, :] < length_block[:, None, None]
    scores = jnp.where(visible, scores, -jnp.inf)
    top_score = lax.optimization_barrier(jnp.max(scores, axis=2, keepdims=True))
    exponent = jnp.exp(scores - top_score)
    softmax_probs = (exponent / lax.optimization_barrier(jnp.sum(exponent, axis=2, keepdims=True))).astype(jnp.bfloat16)
    latent_out = jnp.einsum('rhl,rlc->rhc', softmax_probs.astype(jnp.float32), cache_block.astype(jnp.float32))
    return latent_out.astype(jnp.bfloat16)

def run_expert(operands):
    rows_in, gate_part, up_part, down_part = operands
    wide_rows = rows_in.astype(jnp.float32)
    gate_value = jnp.einsum('md,sdh->msh', wide_rows, gate_part.astype(jnp.float32))
    up_value = jnp.einsum('md,sdh->msh', wide_rows, up_part.astype(jnp.float32))
    hidden = (jax.nn.silu(gate_value) * up_value).astype(jnp.bfloat16)
    shard_out = jnp.einsum('msh,shd->msd', hidden.astype(jnp.float32), down_part.astype(jnp.float32)).astype(jnp.bfloat16)
    shard_out = lax.optimization_barrier(shard_out)
    return lax.optimization_barrier(jnp.sum(shard_out.astype(jnp.float32), axis=1)).astype(jnp.bfloat16)

def reference(q_nope, q_rope, w_absorb_k, latent_cache, rope_keys, cache_lengths, w_absorb_v, w_out, norm_gain, routes, expert_probs, group_probs, w_gate, w_up, w_down):
    query_heads = q_nope.reshape(TOKENS, HEADS, NOPE).astype(jnp.float32)
    query_latent = jnp.einsum('thn,hnc->thc', query_heads, w_absorb_k.astype(jnp.float32)).astype(jnp.bfloat16)
    query_rope = q_rope.reshape(TOKENS, HEADS, ROPE)
    blocks = TOKENS // R_DEV
    operands = (query_latent.reshape(blocks, R_DEV, HEADS, LATENT), query_rope.reshape(blocks, R_DEV, HEADS, ROPE), latent_cache.reshape(blocks, R_DEV, CAP_LEN, LATENT), rope_keys.reshape(blocks, R_DEV, ROPE, CAP_LEN), cache_lengths.reshape(blocks, R_DEV))
    latent_out = lax.map(attend_block, operands).reshape(TOKENS, HEADS, LATENT)
    head_values = jnp.einsum('thc,hcv->thv', latent_out.astype(jnp.float32), w_absorb_v.astype(jnp.float32))
    head_values = head_values.astype(jnp.bfloat16).reshape(TOKENS, HEADS * VHEAD)
    attended = jnp.dot(head_values, w_out, preferred_element_type=jnp.float32).astype(jnp.bfloat16)
    attended_wide = attended.astype(jnp.float32)
    mean_square = lax.optimization_barrier(jnp.mean(attended_wide * attended_wide, axis=1, keepdims=True))
    normed = (attended_wide * lax.rsqrt(mean_square + 1e-06) * norm_gain[None, :]).astype(jnp.bfloat16)
    flat_routes = routes.reshape(blocks, R_DEV * TOPK).astype(jnp.int32)
    chosen = (flat_routes[:, :, None] == jnp.arange(EXPERTS, dtype=jnp.int32)[None, None, :]).astype(jnp.int32)
    earlier = jnp.cumsum(chosen, axis=1) - chosen
    rank_in = lax.optimization_barrier(jnp.sum(earlier * chosen, axis=2)).astype(jnp.int32)
    block_ids = jnp.arange(blocks, dtype=jnp.int32)[:, None]
    slot_index = ((flat_routes * blocks + block_ids) * CAP + rank_in).astype(jnp.int32)
    source_rows = block_ids * R_DEV + jnp.arange(R_DEV * TOPK, dtype=jnp.int32)[None, :] // TOPK
    table = jnp.zeros((EXPERTS * blocks * CAP,), jnp.int32).at[slot_index.reshape(-1)].set(source_rows.reshape(-1).astype(jnp.int32))
    expert_rows = normed[table].reshape(EXPERTS, blocks * CAP, D)
    gate_all = w_gate.reshape(EXPERTS, SHARDS, D, HID_DEV)
    up_all = w_up.reshape(EXPERTS, SHARDS, D, HID_DEV)
    down_all = w_down.reshape(EXPERTS, SHARDS, HID_DEV, D)
    expert_out = lax.map(run_expert, (expert_rows, gate_all, up_all, down_all)).reshape(EXPERTS * blocks * CAP, D)
    pair_rows = expert_out[slot_index.reshape(-1)].reshape(TOKENS, TOPK, D).astype(jnp.float32)
    group_weight = jnp.take_along_axis(group_probs, (routes // EXP_GRP).astype(jnp.int32), axis=1)
    pair_weight = group_weight * expert_probs
    mixed = lax.optimization_barrier(jnp.sum(pair_weight[:, :, None] * pair_rows, axis=1))
    return mixed.astype(jnp.bfloat16)
```

```python
import functools

import jax
import jax.numpy as jnp
from jax import lax
from jax.experimental import pallas as pl
from jax.experimental.pallas import tpu as pltpu
from jax.sharding import PartitionSpec as P

EXP_GRP = 2
CAP = 4
F32 = jnp.float32
BF16 = jnp.bfloat16


def hidden_kernel(count, *refs):
    row_refs = refs[:count]
    gate_ref, up_ref, out_ref, gate_sum, up_sum = refs[count:]
    step = pl.program_id(0)

    @pl.when(step == 0)
    def _():
        gate_sum[...] = jnp.zeros_like(gate_sum)
        up_sum[...] = jnp.zeros_like(up_sum)

    rows = jnp.concatenate([ref[...] for ref in row_refs], axis=0)
    gate_sum[...] += jnp.dot(rows, gate_ref[0], preferred_element_type=F32)
    up_sum[...] += jnp.dot(rows, up_ref[0], preferred_element_type=F32)

    @pl.when(step == pl.num_programs(0) - 1)
    def _():
        gate = gate_sum[...]
        out_ref[...] = (gate * jax.nn.sigmoid(gate) * up_sum[...]).astype(BF16)


def expert_hidden(blocks, w_gate, w_up, tile=1024):
    rows = sum(block.shape[0] for block in blocks)
    width, units = w_gate.shape[1:]
    return pl.pallas_call(
        functools.partial(hidden_kernel, len(blocks)),
        grid=(width // tile,),
        out_shape=jax.ShapeDtypeStruct((rows, units), BF16),
        in_specs=[pl.BlockSpec((block.shape[0], tile), lambda i: (0, i)) for block in blocks]
        + [pl.BlockSpec((1, tile, units), lambda i: (0, i, 0))] * 2,
        out_specs=pl.BlockSpec((rows, units), lambda i: (0, 0)),
        scratch_shapes=[pltpu.VMEM((rows, units), F32)] * 2,
        compiler_params=pltpu.CompilerParams(vmem_limit_bytes=24 * 1024 * 1024),
        cost_estimate=pl.CostEstimate(
            flops=4 * rows * width * units,
            bytes_accessed=2 * width * (2 * units + rows),
            transcendentals=rows * units,
        ),
    )(*blocks, w_gate, w_up)


def per_device(
    q_nope,
    q_rope,
    w_absorb_k,
    latent_cache,
    rope_keys,
    cache_lengths,
    w_absorb_v,
    w_out,
    norm_gain,
    routes,
    expert_probs,
    group_probs,
    w_gate,
    w_up,
    w_down,
):
    batch_rows = q_nope.shape[0]
    heads_local, nope_width, latent_width = w_absorb_k.shape
    rope_width = q_rope.shape[1] // heads_local
    value_width = w_absorb_v.shape[2]
    model_width = w_out.shape[1]
    requests, _, cache_len = rope_keys.shape
    devs = lax.axis_size("dev")
    groups = lax.axis_size("grp")
    shards = devs // EXP_GRP
    experts = EXP_GRP * groups
    top_count = routes.shape[1]
    softmax_scale = float(nope_width + rope_width) ** (-0.5)
    halves = [[half * shards + s for s in range(shards)] for half in range(EXP_GRP)]

    units = w_down.shape[1]
    slice_width = model_width // shards
    down = w_down[0].reshape(units, shards, slice_width).transpose(1, 0, 2)
    down = lax.all_to_all(
        down, "dev", split_axis=0, concat_axis=0, tiled=True, axis_index_groups=halves
    )

    query_heads = q_nope.reshape(batch_rows, heads_local, nope_width)
    query_latent = jnp.einsum("bhn,hnc->bhc", query_heads, w_absorb_k, preferred_element_type=F32)
    query_latent = query_latent.astype(BF16).reshape(batch_rows, heads_local * latent_width)
    query = jnp.concatenate([query_latent, q_rope], axis=1)
    query = query.reshape(devs, requests, query.shape[1])
    query = lax.all_to_all(query, "dev", split_axis=0, concat_axis=0, tiled=True)
    split = heads_local * latent_width
    heads = devs * heads_local
    owner_latent = (
        query[:, :, :split]
        .reshape(devs, requests, heads_local, latent_width)
        .transpose(1, 0, 2, 3)
        .reshape(requests, heads, latent_width)
    )
    owner_rope = (
        query[:, :, split:]
        .reshape(devs, requests, heads_local, rope_width)
        .transpose(1, 0, 2, 3)
        .reshape(requests, heads, rope_width)
    )
    scores = jnp.einsum("rhc,rlc->rhl", owner_latent, latent_cache, preferred_element_type=F32)
    scores = scores + jnp.einsum("rhp,rpl->rhl", owner_rope, rope_keys, preferred_element_type=F32)
    scores = scores * softmax_scale
    visible = jnp.arange(cache_len)[None, None, :] < cache_lengths[:, None, None]
    scores = jnp.where(visible, scores, -jnp.inf)
    top_score = jnp.max(scores, axis=2, keepdims=True)
    exponent = jnp.exp(scores - top_score)
    softmax_probs = (exponent / jnp.sum(exponent, axis=2, keepdims=True)).astype(BF16)
    latent_out = jnp.einsum("rhl,rlc->rhc", softmax_probs, latent_cache, preferred_element_type=F32)
    latent_out = (
        latent_out.astype(BF16)
        .reshape(requests, devs, heads_local * latent_width)
        .transpose(1, 0, 2)
    )
    head_latent = lax.all_to_all(latent_out, "dev", split_axis=0, concat_axis=0, tiled=True)
    head_latent = head_latent.reshape(batch_rows, heads_local, latent_width)
    head_values = jnp.einsum("bhc,hcv->bhv", head_latent, w_absorb_v, preferred_element_type=F32)
    head_values = head_values.astype(BF16).reshape(batch_rows, heads_local * value_width)
    partial = jnp.dot(head_values, w_out, preferred_element_type=F32).astype(BF16)
    partial = lax.all_to_all(
        partial.reshape(devs, requests, model_width),
        "dev",
        split_axis=0,
        concat_axis=0,
        tiled=True,
    )
    attended = jnp.sum(partial.astype(F32), axis=0).astype(BF16)
    attended_wide = attended.astype(F32)
    mean_square = jnp.mean(attended_wide * attended_wide, axis=1, keepdims=True)
    normed = (attended_wide * lax.rsqrt(mean_square + 1e-06) * norm_gain[None, :]).astype(BF16)

    flat_routes = routes.reshape(requests * top_count)
    chosen = (flat_routes[:, None] == jnp.arange(experts)[None, :]).astype(jnp.int32)
    earlier = jnp.cumsum(chosen, axis=0) - chosen
    rank_in = jnp.sum(earlier * chosen, axis=1)
    slot_index = (flat_routes * CAP + rank_in).reshape(requests, top_count)
    slot_ids = jnp.arange(experts * CAP)
    placed = slot_index[None, :, :] == slot_ids[:, None, None]
    dispatch = jnp.any(placed, axis=2).astype(BF16)
    outgoing = jnp.dot(dispatch, normed, preferred_element_type=F32).astype(BF16)

    peers = [
        [g * devs + half * shards + p for g in range(groups) for half in range(EXP_GRP)]
        for p in range(shards)
    ]
    own = lax.all_to_all(
        outgoing.reshape(experts, CAP, model_width),
        ("grp", "dev"),
        split_axis=0,
        concat_axis=0,
        tiled=True,
        axis_index_groups=peers,
    ).reshape(experts * CAP, model_width)

    ring = shards // 2
    z_up = [(i, i // ring * ring + (i + 1) % ring) for i in range(devs)]
    z_down = [(i, i // ring * ring + (i + ring - 1) % ring) for i in range(devs)]
    y_pair = [(i, i ^ ring) for i in range(devs)]
    half_rows = own.shape[0] // 2
    lo, hi = slice(0, half_rows), slice(half_rows, None)

    def send(value, way):
        return lax.ppermute(value, "dev", way)

    below = send(own, z_up)
    above = send(own, z_down)
    beside = send(own, y_pair)
    first = expert_hidden([own, below, above, beside], w_gate, w_up)
    far_lo = send(below[lo], z_up)
    far_hi = send(above[hi], z_down)
    beside_below_lo = send(beside[lo], z_up)
    beside_above_hi = send(beside[hi], z_down)
    beside_below_hi = send(below[hi], y_pair)
    beside_above_lo = send(above[lo], y_pair)
    second = expert_hidden(
        [far_lo, far_hi, beside_below_lo, beside_below_hi, beside_above_lo, beside_above_hi],
        w_gate,
        w_up,
    )
    beside_far_lo = send(beside_below_lo, z_up)
    beside_far_hi = send(beside_above_hi, z_down)
    third = expert_hidden([beside_far_lo, beside_far_hi], w_gate, w_up)
    rows = own.shape[0]
    relative = jnp.concatenate([first, second, third], axis=0).reshape(shards, rows, units)
    order = jnp.array([0, 1, 4, 2, 3, 5, 7, 6], jnp.int32)
    place = lax.axis_index("dev") % shards
    position = jnp.arange(shards, dtype=jnp.int32)
    other = (position // ring) ^ (place // ring)
    steps = (place % ring - position % ring) % ring
    hidden = relative[order[other * ring + steps]].reshape(shards * rows, units)

    everyone = lax.all_to_all(
        jnp.broadcast_to(hidden[None], (shards, shards * rows, units)),
        "dev",
        split_axis=0,
        concat_axis=0,
        tiled=True,
        axis_index_groups=halves,
    )
    result = jnp.einsum("smk,skd->md", everyone, down, preferred_element_type=F32).astype(BF16)
    result = (
        result.reshape(shards, groups, EXP_GRP, CAP, slice_width)
        .transpose(1, 2, 0, 3, 4)
        .reshape(groups * devs, CAP, slice_width)
    )
    result = lax.all_to_all(result, ("grp", "dev"), split_axis=0, concat_axis=0, tiled=True)
    expert_out = (
        result.reshape(experts, shards, CAP, slice_width)
        .transpose(0, 2, 1, 3)
        .reshape(experts * CAP, model_width)
    )
    pair_rows = expert_out[slot_index.reshape(-1)].reshape(requests, top_count, model_width)
    group_match = (routes // EXP_GRP)[:, :, None] == jnp.arange(groups)[None, None, :]
    group_weight = jnp.sum(jnp.where(group_match, group_probs[:, None, :], 0.0), axis=2)
    pair_weight = group_weight * expert_probs
    mixed = jnp.sum(pair_weight[:, :, None] * pair_rows.astype(F32), axis=1)
    return mixed.astype(BF16)


def solution(mesh):
    placed = (
        P("grp", "dev"),
        P("grp", "dev"),
        P("dev", None, None),
        P(("grp", "dev"), None, None),
        P(("grp", "dev"), None, None),
        P(("grp", "dev")),
        P("dev", None, None),
        P("dev", None),
        P(),
        P(("grp", "dev"), None),
        P(("grp", "dev"), None),
        P(("grp", "dev"), None),
        P(("grp", "dev"), None, None),
        P(("grp", "dev"), None, None),
        P(("grp", "dev"), None, None),
    )
    return jax.shard_map(
        per_device, mesh=mesh, in_specs=placed, out_specs=P(("grp", "dev"), None), check_vma=False
    )
```

```python
import functools

import jax
import jax.numpy as jnp
from jax import lax
from jax.experimental import pallas as pl
from jax.experimental.pallas import tpu as pltpu
from jax.sharding import PartitionSpec as P

EXP_GRP = 2
CAP = 4
LIMIT = 56 * 1024 * 1024
F32 = jnp.float32
BF16 = jnp.bfloat16


def hidden_kernel(count, *refs):
    row_refs = refs[:count]
    gate_ref, up_ref, out_ref, gate_sum, up_sum = refs[count:]
    step = pl.program_id(0)

    @pl.when(step == 0)
    def _():
        gate_sum[...] = jnp.zeros_like(gate_sum)
        up_sum[...] = jnp.zeros_like(up_sum)

    rows = jnp.concatenate([ref[...] for ref in row_refs], axis=0)
    gate_sum[...] += jnp.dot(rows, gate_ref[0], preferred_element_type=F32)
    up_sum[...] += jnp.dot(rows, up_ref[0], preferred_element_type=F32)

    @pl.when(step == pl.num_programs(0) - 1)
    def _():
        gate = gate_sum[...]
        out_ref[...] = (gate * jax.nn.sigmoid(gate) * up_sum[...]).astype(BF16)


def expert_hidden(blocks, w_gate, w_up, tile=1024):
    rows = sum(block.shape[0] for block in blocks)
    width, units = w_gate.shape[1:]
    return pl.pallas_call(
        functools.partial(hidden_kernel, len(blocks)),
        grid=(width // tile,),
        out_shape=jax.ShapeDtypeStruct((rows, units), BF16),
        in_specs=[pl.BlockSpec((block.shape[0], tile), lambda i: (0, i)) for block in blocks]
        + [pl.BlockSpec((1, tile, units), lambda i: (0, i, 0))] * 2,
        out_specs=pl.BlockSpec((rows, units), lambda i: (0, 0)),
        scratch_shapes=[pltpu.VMEM((rows, units), F32)] * 2,
        compiler_params=pltpu.CompilerParams(vmem_limit_bytes=24 * 1024 * 1024),
        cost_estimate=pl.CostEstimate(
            flops=4 * rows * width * units,
            bytes_accessed=2 * width * (2 * units + rows),
            transcendentals=rows * units,
        ),
    )(*blocks, w_gate, w_up)


def relay_kernel(count, order_ref, weight_ref, *refs):
    out_refs, held, in_sems, out_sems = refs[:count], *refs[count:]
    width = out_refs[0].shape[1]
    arriving, leaving = [], []
    for k in range(count):
        start = pl.multiple_of(order_ref[k] * width, 128)
        copy = pltpu.make_async_copy(
            weight_ref.at[0, :, pl.ds(start, width)], held.at[k], in_sems.at[k]
        )
        copy.start()
        arriving.append(copy)
    for k in range(count):
        arriving[k].wait()
        copy = pltpu.make_async_copy(held.at[k], out_refs[k], out_sems.at[k])
        copy.start()
        leaving.append(copy)
    for copy in leaving:
        copy.wait()


def column_blocks(weight, order):
    _, rows, columns = weight.shape
    count = order.shape[0]
    width = columns // count
    return pl.pallas_call(
        functools.partial(relay_kernel, count),
        out_shape=[jax.ShapeDtypeStruct((rows, width), weight.dtype)] * count,
        in_specs=[pl.BlockSpec(memory_space=pltpu.SMEM), pl.BlockSpec(memory_space=pl.ANY)],
        out_specs=[pl.BlockSpec(memory_space=pl.ANY)] * count,
        scratch_shapes=[
            pltpu.VMEM((count, rows, width), weight.dtype),
            pltpu.SemaphoreType.DMA((count,)),
            pltpu.SemaphoreType.DMA((count,)),
        ],
        compiler_params=pltpu.CompilerParams(vmem_limit_bytes=LIMIT),
        cost_estimate=pl.CostEstimate(
            flops=0, bytes_accessed=4 * rows * columns, transcendentals=0
        ),
    )(order, weight)


def down_kernel(groups, order_ref, hidden_ref, *refs):
    ring, total, units = hidden_ref.shape
    pieces = len(refs) - 3
    down_refs, out_ref, down, sems = refs[:pieces], *refs[pieces:]
    width = down_refs[0].shape[1]
    share = pieces // ring
    copies = [
        pltpu.make_async_copy(
            down_refs[i],
            down.at[pl.ds(i // share * units, units), pl.ds(i % share * width, width)],
            sems.at[i],
        )
        for i in range(pieces)
    ]
    for copy in copies:
        copy.start()
    for copy in copies:
        copy.wait()
    peers = groups * EXP_GRP
    rows = peers * CAP
    places = total // rows
    parts = 2
    tall = total // parts
    for part in range(parts):
        hidden = jnp.concatenate(
            [hidden_ref[order_ref[k], part * tall : (part + 1) * tall] for k in range(ring)],
            axis=1,
        )
        value = jnp.dot(hidden, down[...], preferred_element_type=F32).astype(BF16)
        for place in range(places // parts):
            for peer in range(peers):
                row = place * rows + peer * CAP
                out_ref[peer * places + part * (places // parts) + place] = value[row : row + CAP]


def expert_down(hidden, down, order, groups):
    ring, rows, units = hidden.shape
    width = down[0].shape[1] * len(down) // ring
    return pl.pallas_call(
        functools.partial(down_kernel, groups),
        out_shape=jax.ShapeDtypeStruct((rows // CAP, CAP, width), BF16),
        in_specs=[
            pl.BlockSpec(memory_space=pltpu.SMEM),
            pl.BlockSpec(memory_space=pltpu.VMEM),
        ]
        + [pl.BlockSpec(memory_space=pl.ANY)] * len(down),
        out_specs=pl.BlockSpec(memory_space=pltpu.VMEM),
        scratch_shapes=[
            pltpu.VMEM((ring * units, width), BF16),
            pltpu.SemaphoreType.DMA((len(down),)),
        ],
        compiler_params=pltpu.CompilerParams(vmem_limit_bytes=LIMIT),
        cost_estimate=pl.CostEstimate(
            flops=2 * ring * rows * units * width,
            bytes_accessed=2 * (ring * units * (rows + width) + rows * width),
            transcendentals=0,
        ),
    )(order, hidden, *down)


def absorb_kernel(nope_ref, rope_ref, weight_ref, out_ref, nope, rope, weight, sems):
    copies = [
        pltpu.make_async_copy(source, target, sems.at[i])
        for i, (source, target) in enumerate(
            ((nope_ref, nope), (weight_ref, weight), (rope_ref, rope))
        )
    ]
    for copy in copies:
        copy.start()
    copies[0].wait()
    copies[1].wait()
    heads, width, latent = weight.shape
    for h in range(heads):
        out_ref[:, h * latent : (h + 1) * latent] = jnp.dot(
            nope[:, h * width : (h + 1) * width], weight[h], preferred_element_type=F32
        ).astype(BF16)
    copies[2].wait()
    out_ref[:, heads * latent :] = rope[...]


def absorb(q_nope, q_rope, w_absorb_k):
    rows = q_nope.shape[0]
    heads, width, latent = w_absorb_k.shape
    columns = heads * latent + q_rope.shape[1]
    return pl.pallas_call(
        absorb_kernel,
        out_shape=jax.ShapeDtypeStruct((rows, columns), BF16),
        in_specs=[pl.BlockSpec(memory_space=pl.ANY)] * 3,
        out_specs=pl.BlockSpec(memory_space=pltpu.VMEM),
        scratch_shapes=[
            pltpu.VMEM(q_nope.shape, BF16),
            pltpu.VMEM(q_rope.shape, BF16),
            pltpu.VMEM(w_absorb_k.shape, BF16),
            pltpu.SemaphoreType.DMA((3,)),
        ],
        compiler_params=pltpu.CompilerParams(vmem_limit_bytes=LIMIT),
        cost_estimate=pl.CostEstimate(
            flops=2 * rows * heads * width * latent,
            bytes_accessed=2 * (rows * columns + heads * width * latent),
            transcendentals=0,
        ),
    )(q_nope, q_rope, w_absorb_k)


def attend_kernel(heads, scale, length_ref, query_ref, cache_ref, keys_ref, out_ref, wide, total):
    request = pl.program_id(0)
    devs = query_ref.shape[0]
    latent = cache_ref.shape[2]
    rope = keys_ref.shape[1]

    @pl.when(request == 0)
    def _():
        wide[...] = query_ref[...].astype(F32)

    query = wide[:, pl.ds(request, 1), :].reshape(devs, wide.shape[2]).astype(BF16)
    split = heads * latent
    parts = [query[:, h * latent : (h + 1) * latent] for h in range(heads)]
    ropes = [query[:, split + h * rope : split + (h + 1) * rope] for h in range(heads)]
    cache = cache_ref[0]
    scores = lax.dot_general(
        jnp.concatenate(parts, axis=0),
        cache,
        (((1,), (1,)), ((), ())),
        preferred_element_type=F32,
    )
    scores += jnp.dot(jnp.concatenate(ropes, axis=0), keys_ref[0], preferred_element_type=F32)
    scores *= scale
    live = lax.broadcasted_iota(jnp.int32, scores.shape, 1) < length_ref[request]
    scores = jnp.where(live, scores, -jnp.inf)
    exponent = jnp.exp(scores - jnp.max(scores, axis=1, keepdims=True))
    probs = (exponent / jnp.sum(exponent, axis=1, keepdims=True)).astype(BF16)
    value = jnp.dot(probs, cache, preferred_element_type=F32)
    value = jnp.concatenate([value[h * devs : (h + 1) * devs] for h in range(heads)], axis=1)
    total[:, pl.ds(request, 1), :] = value.reshape(devs, 1, split)

    @pl.when(request == pl.num_programs(0) - 1)
    def _():
        out_ref[...] = total[...].astype(BF16)


def attend(query, latent_cache, rope_keys, lengths, heads, scale):
    devs, requests, columns = query.shape
    _, rope, positions = rope_keys.shape
    latent = latent_cache.shape[2]
    rows = heads * devs
    return pl.pallas_call(
        functools.partial(attend_kernel, heads, scale),
        grid=(requests,),
        out_shape=jax.ShapeDtypeStruct((devs, requests, heads * latent), BF16),
        in_specs=[
            pl.BlockSpec(memory_space=pltpu.SMEM),
            pl.BlockSpec((devs, requests, columns), lambda r: (0, 0, 0)),
            pl.BlockSpec((1, positions, latent), lambda r: (r, 0, 0)),
            pl.BlockSpec((1, rope, positions), lambda r: (r, 0, 0)),
        ],
        out_specs=pl.BlockSpec((devs, requests, heads * latent), lambda r: (0, 0, 0)),
        scratch_shapes=[
            pltpu.VMEM((devs, requests, columns), F32),
            pltpu.VMEM((devs, requests, heads * latent), F32),
        ],
        compiler_params=pltpu.CompilerParams(vmem_limit_bytes=10 * 1024 * 1024),
        cost_estimate=pl.CostEstimate(
            flops=2 * requests * rows * positions * (2 * latent + rope),
            bytes_accessed=2 * requests * positions * (latent + rope),
            transcendentals=requests * rows * positions,
        ),
    )(lengths, query, latent_cache, rope_keys)


def project_kernel(latent_ref, absorb_hbm, weight_hbm, out_ref, absorb_ref, weight, sems):
    heads, latent, width = absorb_ref.shape
    tiles = sems.shape[0] - 1
    tile = weight.shape[1] // tiles
    copies = [pltpu.make_async_copy(absorb_hbm, absorb_ref, sems.at[tiles])] + [
        pltpu.make_async_copy(
            weight_hbm.at[:, pl.ds(t * tile, tile)], weight.at[:, pl.ds(t * tile, tile)], sems.at[t]
        )
        for t in range(tiles)
    ]
    for copy in copies:
        copy.start()
    copies[0].wait()
    values = jnp.concatenate(
        [
            jnp.dot(
                latent_ref[:, h * latent : (h + 1) * latent],
                absorb_ref[h],
                preferred_element_type=F32,
            ).astype(BF16)
            for h in range(heads)
        ],
        axis=1,
    )
    for t in range(tiles):
        copies[t + 1].wait()
        out_ref[:, t * tile : (t + 1) * tile] = jnp.dot(
            values, weight[:, t * tile : (t + 1) * tile], preferred_element_type=F32
        ).astype(BF16)


def project(head_latent, w_absorb_v, w_out, tiles=7):
    rows = head_latent.shape[0]
    depth, columns = w_out.shape
    return pl.pallas_call(
        project_kernel,
        out_shape=jax.ShapeDtypeStruct((rows, columns), BF16),
        in_specs=[
            pl.BlockSpec(memory_space=pltpu.VMEM),
            pl.BlockSpec(memory_space=pl.ANY),
            pl.BlockSpec(memory_space=pl.ANY),
        ],
        out_specs=pl.BlockSpec(memory_space=pltpu.VMEM),
        scratch_shapes=[
            pltpu.VMEM(w_absorb_v.shape, BF16),
            pltpu.VMEM(w_out.shape, BF16),
            pltpu.SemaphoreType.DMA((tiles + 1,)),
        ],
        compiler_params=pltpu.CompilerParams(vmem_limit_bytes=LIMIT),
        cost_estimate=pl.CostEstimate(
            flops=2 * rows * (depth * columns + w_absorb_v.size),
            bytes_accessed=2 * (depth * columns + rows * columns),
            transcendentals=0,
        ),
    )(head_latent, w_absorb_v, w_out)


def dispatch_kernel(partial_ref, gain_ref, place_ref, out_ref, wide):
    devs, requests, width = partial_ref.shape
    tile = width // 8
    square = jnp.zeros((requests, 1), F32)
    for t in range(0, width, tile):
        total = partial_ref[0, :, t : t + tile].astype(F32)
        for d in range(1, devs):
            total += partial_ref[d, :, t : t + tile].astype(F32)
        attended = total.astype(BF16).astype(F32)
        wide[:, t : t + tile] = attended
        square += jnp.sum(attended * attended, axis=1, keepdims=True)
    factor = lax.rsqrt(square / width + 1e-06)
    for t in range(0, width, tile):
        normed = (wide[:, t : t + tile] * factor * gain_ref[:, t : t + tile]).astype(BF16)
        rows = jnp.dot(place_ref[...], normed, preferred_element_type=F32).astype(BF16)
        for e in range(out_ref.shape[0]):
            out_ref[e, :, t : t + tile] = rows[e * CAP : (e + 1) * CAP]


def dispatch_rows(partial, gain, place):
    _, requests, width = partial.shape
    slots = place.shape[0]
    return pl.pallas_call(
        dispatch_kernel,
        out_shape=jax.ShapeDtypeStruct((slots // CAP, CAP, width), BF16),
        in_specs=[pl.BlockSpec(memory_space=pltpu.VMEM)] * 3,
        out_specs=pl.BlockSpec(memory_space=pltpu.VMEM),
        scratch_shapes=[pltpu.VMEM((requests, width), F32)],
        compiler_params=pltpu.CompilerParams(vmem_limit_bytes=10 * 1024 * 1024),
        cost_estimate=pl.CostEstimate(
            flops=2 * slots * requests * width,
            bytes_accessed=2 * partial.size,
            transcendentals=0,
        ),
    )(partial, gain, place)


def mix_kernel(ring, weight_ref, rows_ref, out_ref):
    width = rows_ref.shape[2]
    slots = weight_ref.shape[1]
    experts = slots // CAP
    shards = rows_ref.shape[0] // experts
    for z in range(ring):
        rows = jnp.concatenate(
            [
                sum(rows_ref[e * shards + s].astype(F32) for s in range(z, shards, ring))
                for e in range(experts)
            ],
            axis=0,
        )
        out_ref[:, z * width : (z + 1) * width] = jnp.dot(
            weight_ref[...], rows, precision=lax.Precision.HIGHEST, preferred_element_type=F32
        ).astype(BF16)


def mix(weight, rows, ring):
    requests, slots = weight.shape
    width = rows.shape[2]
    return pl.pallas_call(
        functools.partial(mix_kernel, ring),
        out_shape=jax.ShapeDtypeStruct((requests, ring * width), BF16),
        in_specs=[pl.BlockSpec(memory_space=pltpu.VMEM)] * 2,
        out_specs=pl.BlockSpec(memory_space=pltpu.VMEM),
        compiler_params=pltpu.CompilerParams(vmem_limit_bytes=10 * 1024 * 1024),
        cost_estimate=pl.CostEstimate(
            flops=2 * requests * slots * ring * width,
            bytes_accessed=2 * rows.size,
            transcendentals=0,
        ),
    )(weight, rows)


def per_device(
    q_nope,
    q_rope,
    w_absorb_k,
    latent_cache,
    rope_keys,
    cache_lengths,
    w_absorb_v,
    w_out,
    norm_gain,
    routes,
    expert_probs,
    group_probs,
    w_gate,
    w_up,
    w_down,
):
    batch_rows = q_nope.shape[0]
    heads_local, nope_width, latent_width = w_absorb_k.shape
    rope_width = q_rope.shape[1] // heads_local
    model_width = w_out.shape[1]
    requests, _, cache_len = rope_keys.shape
    devs = lax.axis_size("dev")
    groups = lax.axis_size("grp")
    shards = devs // EXP_GRP
    experts = EXP_GRP * groups
    top_count = routes.shape[1]
    softmax_scale = float(nope_width + rope_width) ** (-0.5)

    ring = shards // 2
    z_up = [(i, i // ring * ring + (i + 1) % ring) for i in range(devs)]
    z_down = [(i, i // ring * ring + (i + ring - 1) % ring) for i in range(devs)]
    y_pair = [(i, i ^ ring) for i in range(devs)]

    units = w_down.shape[1]
    place = lax.axis_index("dev") % shards
    step = jnp.arange(ring, dtype=jnp.int32)
    targets = (place + step) % ring
    sources = (place + ring - step) % ring
    split = shards // ring
    down_out = column_blocks(
        w_down, (targets[:, None] * split + jnp.arange(split, dtype=jnp.int32)).reshape(shards)
    )

    def relay(k, half):
        way = [(i, i // ring * ring + (i + k) % ring) for i in range(devs)]
        return lax.ppermute(down_out[k * split + half], "dev", way)

    query = absorb(q_nope, q_rope, w_absorb_k)
    query = query.reshape(devs, requests, query.shape[1])
    query = lax.all_to_all(query, "dev", split_axis=0, concat_axis=0, tiled=True)
    down = {(0, half): down_out[half] for half in range(split)}
    down |= {(1, 0): relay(1, 0), (3, 0): relay(3, 0)}
    latent_out = attend(
        query, latent_cache, rope_keys, cache_lengths, heads_local, softmax_scale
    )
    latent_out, down, down_out = lax.optimization_barrier((latent_out, down, down_out))
    down |= {(1, 1): relay(1, 1), (3, 1): relay(3, 1)}
    head_latent = lax.all_to_all(latent_out, "dev", split_axis=0, concat_axis=0, tiled=True)
    partial = project(
        head_latent.reshape(batch_rows, heads_local * latent_width), w_absorb_v, w_out
    )
    partial, down, down_out = lax.optimization_barrier((partial, down, down_out))
    partial = lax.all_to_all(
        partial.reshape(devs, requests, model_width),
        "dev",
        split_axis=0,
        concat_axis=0,
        tiled=True,
    )
    partial, down_out = lax.optimization_barrier((partial, down_out))
    down |= {(2, 0): relay(2, 0), (2, 1): relay(2, 1)}

    flat_routes = routes.reshape(requests * top_count)
    chosen = (flat_routes[:, None] == jnp.arange(experts)[None, :]).astype(jnp.int32)
    earlier = jnp.cumsum(chosen, axis=0) - chosen
    rank_in = jnp.sum(earlier * chosen, axis=1)
    slot_index = (flat_routes * CAP + rank_in).reshape(requests, top_count)
    slot_ids = jnp.arange(experts * CAP)
    placed = slot_index[None, :, :] == slot_ids[:, None, None]
    dispatch = jnp.any(placed, axis=2).astype(BF16)
    group_match = (routes // EXP_GRP)[:, :, None] == jnp.arange(groups)[None, None, :]
    group_weight = jnp.sum(jnp.where(group_match, group_probs[:, None, :], 0.0), axis=2)
    pair_weight = group_weight * expert_probs
    slot_weight = jnp.sum(jnp.where(placed, pair_weight[None], 0.0), axis=2).T
    outgoing = dispatch_rows(partial, norm_gain[None, :], dispatch)

    peers = [
        [g * devs + half * shards + p for g in range(groups) for half in range(EXP_GRP)]
        for p in range(shards)
    ]
    own = lax.all_to_all(
        outgoing,
        ("grp", "dev"),
        split_axis=0,
        concat_axis=0,
        tiled=True,
        axis_index_groups=peers,
    ).reshape(experts * CAP, model_width)

    own, down = lax.optimization_barrier((own, down))

    half_rows = own.shape[0] // 2
    lo, hi = slice(0, half_rows), slice(half_rows, None)

    def send(value, way):
        return lax.ppermute(value, "dev", way)

    below = send(own, z_up)
    above = send(own, z_down)
    beside = send(own, y_pair)
    first = expert_hidden([own, below, above, beside], w_gate, w_up)
    far_lo = send(below[lo], z_up)
    far_hi = send(above[hi], z_down)
    beside_below_lo = send(beside[lo], z_up)
    beside_above_hi = send(beside[hi], z_down)
    beside_below_hi = send(below[hi], y_pair)
    beside_above_lo = send(above[lo], y_pair)
    second = expert_hidden(
        [far_lo, far_hi, beside_below_lo, beside_below_hi, beside_above_lo, beside_above_hi],
        w_gate,
        w_up,
    )
    beside_far_lo = send(beside_below_lo, z_up)
    beside_far_hi = send(beside_above_hi, z_down)
    beside_far_lo, beside_far_hi, first, second = lax.optimization_barrier(
        (beside_far_lo, beside_far_hi, first, second)
    )
    third = expert_hidden([beside_far_lo, beside_far_hi], w_gate, w_up)
    rows = own.shape[0]
    relative = jnp.concatenate([first, second, third], axis=0).reshape(shards, rows, units)
    order = jnp.array([0, 1, 4, 2, 3, 5, 7, 6], jnp.int32)
    position = jnp.arange(shards, dtype=jnp.int32)
    other = (position // ring) ^ (place // ring)
    steps = (place % ring - position % ring) % ring
    hidden = relative[order[other * ring + steps]].reshape(shards * rows, units)
    everyone = jnp.broadcast_to(hidden[None], (ring, shards * rows, units))
    rings = [[start + z for z in range(ring)] for start in range(0, devs, ring)]
    everyone = lax.all_to_all(
        everyone, "dev", split_axis=0, concat_axis=0, tiled=True, axis_index_groups=rings
    )
    result = expert_down(
        everyone,
        [down[k, half] for k in range(ring) for half in range(split)],
        sources,
        groups,
    )
    result = lax.all_to_all(result, ("grp", "dev"), split_axis=0, concat_axis=0, tiled=True)
    return mix(slot_weight, result, ring)


def solution(mesh):
    placed = (
        P("grp", "dev"),
        P("grp", "dev"),
        P("dev", None, None),
        P(("grp", "dev"), None, None),
        P(("grp", "dev"), None, None),
        P(("grp", "dev")),
        P("dev", None, None),
        P("dev", None),
        P(),
        P(("grp", "dev"), None),
        P(("grp", "dev"), None),
        P(("grp", "dev"), None),
        P(("grp", "dev"), None, None),
        P(("grp", "dev"), None, None),
        P(("grp", "dev"), None, None),
    )
    return jax.shard_map(
        per_device, mesh=mesh, in_specs=placed, out_specs=P(("grp", "dev"), None), check_vma=False
    )
```

```python
import functools

import jax
import jax.numpy as jnp
from jax import lax
from jax.experimental import pallas as pl
from jax.experimental.pallas import tpu as pltpu
from jax.sharding import PartitionSpec as P

EXP_GRP = 2
CAP = 4
LIMIT = 56 * 1024 * 1024
F32 = jnp.float32
BF16 = jnp.bfloat16


def hidden_kernel(count, *refs):
    row_refs = refs[:count]
    gate_ref, up_ref, out_ref, gate_sum, up_sum = refs[count:]
    step = pl.program_id(0)

    @pl.when(step == 0)
    def _():
        gate_sum[...] = jnp.zeros_like(gate_sum)
        up_sum[...] = jnp.zeros_like(up_sum)

    rows = jnp.concatenate([ref[...] for ref in row_refs], axis=0)
    gate_sum[...] += jnp.dot(rows, gate_ref[0], preferred_element_type=F32)
    up_sum[...] += jnp.dot(rows, up_ref[0], preferred_element_type=F32)

    @pl.when(step == pl.num_programs(0) - 1)
    def _():
        gate = gate_sum[...]
        out_ref[...] = (gate * jax.nn.sigmoid(gate) * up_sum[...]).astype(BF16)


def expert_hidden(blocks, w_gate, w_up, tile=1024):
    rows = sum(block.shape[0] for block in blocks)
    width, units = w_gate.shape[1:]
    return pl.pallas_call(
        functools.partial(hidden_kernel, len(blocks)),
        grid=(width // tile,),
        out_shape=jax.ShapeDtypeStruct((rows, units), BF16),
        in_specs=[pl.BlockSpec((block.shape[0], tile), lambda i: (0, i)) for block in blocks]
        + [pl.BlockSpec((1, tile, units), lambda i: (0, i, 0))] * 2,
        out_specs=pl.BlockSpec((rows, units), lambda i: (0, 0)),
        scratch_shapes=[pltpu.VMEM((rows, units), F32)] * 2,
        compiler_params=pltpu.CompilerParams(vmem_limit_bytes=24 * 1024 * 1024),
        cost_estimate=pl.CostEstimate(
            flops=4 * rows * width * units,
            bytes_accessed=2 * width * (2 * units + rows),
            transcendentals=rows * units,
        ),
    )(*blocks, w_gate, w_up)


def relay_kernel(layout, ring, weight_ref, *refs):
    count = len(layout)
    width = weight_ref.shape[2] // (2 * ring)
    place = lax.axis_index("dev") % ring
    out_refs, held, in_sems, out_sems = refs[:count], *refs[count:]
    arriving, leaving, offset = [], [], 0
    for k in range(count):
        size = out_refs[k].shape[1]
        part = held.at[:, pl.ds(offset, size)]
        block, half = layout[k]
        target = (place + block) % ring
        start = pl.multiple_of((2 * target + half) * width, 128)
        arriving.append(
            pltpu.make_async_copy(weight_ref.at[0, :, pl.ds(start, size)], part, in_sems.at[k])
        )
        leaving.append(pltpu.make_async_copy(part, out_refs[k], out_sems.at[k]))
        offset += size
    for copy in arriving:
        copy.start()
    for k in range(count):
        arriving[k].wait()
        leaving[k].start()
    for copy in leaving:
        copy.wait()


def column_blocks(weight, layout, ring, widths):
    _, rows, columns = weight.shape
    count = len(widths)
    return pl.pallas_call(
        functools.partial(relay_kernel, layout, ring),
        out_shape=[jax.ShapeDtypeStruct((rows, width), weight.dtype) for width in widths],
        in_specs=[pl.BlockSpec(memory_space=pltpu.HBM)],
        out_specs=[pl.BlockSpec(memory_space=pltpu.HBM)] * count,
        scratch_shapes=[
            pltpu.VMEM((rows, columns), weight.dtype),
            pltpu.SemaphoreType.DMA((count,)),
            pltpu.SemaphoreType.DMA((count,)),
        ],
        compiler_params=pltpu.CompilerParams(vmem_limit_bytes=LIMIT),
        cost_estimate=pl.CostEstimate(
            flops=0, bytes_accessed=4 * rows * columns, transcendentals=0
        ),
    )(weight)


def down_kernel(groups, layout, hidden_ref, *refs):
    ring, total, units = hidden_ref.shape
    count = len(layout)
    down_refs, out_ref, hidden, down, hidden_sems, sems = refs[:count], *refs[count:]
    halves = sems.shape[0]
    width = out_ref.shape[2] // halves
    place = lax.axis_index("dev") % ring
    hidden_copies = [
        pltpu.make_async_copy(
            hidden_ref.at[(place + ring - k) % ring],
            hidden.at[:, pl.ds(k * units, units)],
            hidden_sems.at[k],
        )
        for k in range(ring)
    ]
    down_copies = [[] for _ in range(halves)]
    for ref, (k, first) in zip(down_refs, layout):
        for half in range(first, first + ref.shape[1] // width):
            down_copies[half].append(
                pltpu.make_async_copy(
                    ref.at[:, pl.ds((half - first) * width, width)],
                    down.at[pl.ds(k * units, units), pl.ds(half * width, width)],
                    sems.at[half, k],
                )
            )
    for copy in hidden_copies + [copy for part in down_copies for copy in part]:
        copy.start()
    for copy in hidden_copies:
        copy.wait()
    peers = groups * EXP_GRP
    rows = peers * CAP
    places = total // rows
    for half in range(halves):
        for copy in down_copies[half]:
            copy.wait()
        columns = slice(half * width, (half + 1) * width)
        value = jnp.dot(hidden[...], down[:, columns], preferred_element_type=F32).astype(BF16)
        for place in range(places):
            for peer in range(peers):
                row = place * rows + peer * CAP
                out_ref[peer * places + place, :, columns] = value[row : row + CAP]


def expert_down(hidden, down, layout, groups, halves):
    ring, rows, units = hidden.shape
    width = sum(piece.shape[1] for piece in down) // ring
    return pl.pallas_call(
        functools.partial(down_kernel, groups, layout),
        out_shape=jax.ShapeDtypeStruct((rows // CAP, CAP, width), BF16),
        in_specs=[pl.BlockSpec(memory_space=pltpu.VMEM)]
        + [pl.BlockSpec(memory_space=pltpu.HBM)] * len(down),
        out_specs=pl.BlockSpec(memory_space=pltpu.VMEM),
        scratch_shapes=[
            pltpu.VMEM((rows, ring * units), BF16),
            pltpu.VMEM((ring * units, width), BF16),
            pltpu.SemaphoreType.DMA((ring,)),
            pltpu.SemaphoreType.DMA((halves, ring)),
        ],
        compiler_params=pltpu.CompilerParams(vmem_limit_bytes=24 * 1024 * 1024),
        cost_estimate=pl.CostEstimate(
            flops=2 * ring * rows * units * width,
            bytes_accessed=2 * (ring * units * (rows + width) + rows * width),
            transcendentals=0,
        ),
    )(hidden, *down)


def absorb_kernel(nope_ref, rope_ref, weight_ref, out_ref, nope, rope, weight, sems):
    copies = [
        pltpu.make_async_copy(source, target, sems.at[i])
        for i, (source, target) in enumerate(
            ((nope_ref, nope), (weight_ref, weight), (rope_ref, rope))
        )
    ]
    for copy in copies:
        copy.start()
    copies[0].wait()
    copies[1].wait()
    heads, width, latent = weight.shape
    for h in range(heads):
        out_ref[:, h * latent : (h + 1) * latent] = jnp.dot(
            nope[:, h * width : (h + 1) * width], weight[h], preferred_element_type=F32
        ).astype(BF16)
    copies[2].wait()
    out_ref[:, heads * latent :] = rope[...]


def absorb(q_nope, q_rope, w_absorb_k):
    rows = q_nope.shape[0]
    heads, width, latent = w_absorb_k.shape
    columns = heads * latent + q_rope.shape[1]
    return pl.pallas_call(
        absorb_kernel,
        out_shape=jax.ShapeDtypeStruct((rows, columns), BF16),
        in_specs=[pl.BlockSpec(memory_space=pltpu.HBM)] * 3,
        out_specs=pl.BlockSpec(memory_space=pltpu.VMEM),
        scratch_shapes=[
            pltpu.VMEM(q_nope.shape, BF16),
            pltpu.VMEM(q_rope.shape, BF16),
            pltpu.VMEM(w_absorb_k.shape, BF16),
            pltpu.SemaphoreType.DMA((3,)),
        ],
        compiler_params=pltpu.CompilerParams(vmem_limit_bytes=LIMIT),
        cost_estimate=pl.CostEstimate(
            flops=2 * rows * heads * width * latent,
            bytes_accessed=2 * (rows * columns + heads * width * latent),
            transcendentals=0,
        ),
    )(q_nope, q_rope, w_absorb_k)


def attend_kernel(heads, scale, length_ref, query_ref, cache_hbm, keys_hbm, weight_hbm, *refs):
    out_ref, weight_ref, cache_ref, keys_ref, queries, values, sems = refs
    devs, requests, columns = query_ref.shape
    rope = keys_ref.shape[1]
    latent = cache_ref.shape[2]
    rows = devs * requests
    keys_copy = pltpu.make_async_copy(keys_hbm, keys_ref, sems.at[requests])
    cache_copies = [
        pltpu.make_async_copy(cache_hbm.at[r], cache_ref.at[r], sems.at[r])
        for r in range(requests)
    ]
    keys_copy.start()
    for copy in cache_copies:
        copy.start()
    weight_copy = pltpu.make_async_copy(weight_hbm, weight_ref, sems.at[requests + 1])
    weight_copy.start()
    row = lax.broadcasted_iota(jnp.int32, (rows, rows), 0)
    column = lax.broadcasted_iota(jnp.int32, (rows, rows), 1)
    by_request = (column == row % devs * requests + row // devs).astype(BF16)
    by_device = (column == row % requests * devs + row // requests).astype(BF16)
    queries[...] = jnp.dot(
        by_request, query_ref[...].reshape(rows, columns), preferred_element_type=F32
    ).astype(BF16)
    split = heads * latent
    keys_copy.wait()
    group = 4
    for first in range(0, requests, group):
        members = range(first, first + group)
        for r in members:
            cache_copies[r].wait()
        scores = []
        for r in members:
            mine = slice(r * devs, (r + 1) * devs)
            latents = jnp.concatenate(
                [queries[mine, h * latent : (h + 1) * latent] for h in range(heads)], axis=0
            )
            ropes = jnp.concatenate(
                [queries[mine, split + h * rope : split + (h + 1) * rope] for h in range(heads)],
                axis=0,
            )
            scores.append(
                lax.dot_general(
                    latents, cache_ref[r], (((1,), (1,)), ((), ())), preferred_element_type=F32
                )
                + jnp.dot(ropes, keys_ref[r], preferred_element_type=F32)
            )
        probs = []
        for r, score in zip(members, scores):
            live = lax.broadcasted_iota(jnp.int32, score.shape, 1) < length_ref[r]
            score = jnp.where(live, score * scale, -jnp.inf)
            exponent = jnp.exp(score - jnp.max(score, axis=1, keepdims=True))
            probs.append((exponent / jnp.sum(exponent, axis=1, keepdims=True)).astype(BF16))
        for r, prob in zip(members, probs):
            value = jnp.dot(prob, cache_ref[r], preferred_element_type=F32).astype(BF16)
            for h in range(heads):
                values[r * devs : (r + 1) * devs, h * latent : (h + 1) * latent] = value[
                    h * devs : (h + 1) * devs
                ]
    out_ref[...] = (
        jnp.dot(by_device, values[...], preferred_element_type=F32)
        .astype(BF16)
        .reshape(out_ref.shape)
    )
    weight_copy.wait()


def attend(query, latent_cache, rope_keys, lengths, w_out, heads, scale):
    devs, requests, columns = query.shape
    _, rope, positions = rope_keys.shape
    latent = latent_cache.shape[2]
    rows = heads * devs
    return pl.pallas_call(
        functools.partial(attend_kernel, heads, scale),
        out_shape=[
            jax.ShapeDtypeStruct((devs, requests, heads * latent), BF16),
            jax.ShapeDtypeStruct(w_out.shape, BF16),
        ],
        in_specs=[
            pl.BlockSpec(memory_space=pltpu.SMEM),
            pl.BlockSpec(memory_space=pltpu.VMEM),
            pl.BlockSpec(memory_space=pltpu.HBM),
            pl.BlockSpec(memory_space=pltpu.HBM),
            pl.BlockSpec(memory_space=pltpu.HBM),
        ],
        out_specs=[pl.BlockSpec(memory_space=pltpu.VMEM)] * 2,
        scratch_shapes=[
            pltpu.VMEM(latent_cache.shape, BF16),
            pltpu.VMEM(rope_keys.shape, BF16),
            pltpu.VMEM((devs * requests, columns), BF16),
            pltpu.VMEM((devs * requests, heads * latent), BF16),
            pltpu.SemaphoreType.DMA((requests + 2,)),
        ],
        compiler_params=pltpu.CompilerParams(vmem_limit_bytes=28 * 1024 * 1024),
        cost_estimate=pl.CostEstimate(
            flops=2 * requests * rows * positions * (2 * latent + rope),
            bytes_accessed=2 * requests * positions * (latent + rope),
            transcendentals=requests * rows * positions,
        ),
    )(lengths, query, latent_cache, rope_keys, w_out)


def project_kernel(latent_ref, absorb_ref, weight_ref, out_ref):
    heads, latent, _ = absorb_ref.shape
    values = jnp.concatenate(
        [
            jnp.dot(
                latent_ref[:, h * latent : (h + 1) * latent],
                absorb_ref[h],
                preferred_element_type=F32,
            ).astype(BF16)
            for h in range(heads)
        ],
        axis=1,
    )
    tile = 1024
    for t in range(0, weight_ref.shape[1], tile):
        out_ref[:, t : t + tile] = jnp.dot(
            values, weight_ref[:, t : t + tile], preferred_element_type=F32
        ).astype(BF16)


def project(head_latent, w_absorb_v, w_out):
    rows = head_latent.shape[0]
    depth, columns = w_out.shape
    return pl.pallas_call(
        project_kernel,
        out_shape=jax.ShapeDtypeStruct((rows, columns), BF16),
        in_specs=[pl.BlockSpec(memory_space=pltpu.VMEM)] * 3,
        out_specs=pl.BlockSpec(memory_space=pltpu.VMEM),
        compiler_params=pltpu.CompilerParams(vmem_limit_bytes=24 * 1024 * 1024),
        cost_estimate=pl.CostEstimate(
            flops=2 * rows * (depth * columns + w_absorb_v.size),
            bytes_accessed=2 * (depth * columns + rows * columns),
            transcendentals=0,
        ),
    )(head_latent, w_absorb_v, w_out)


def dispatch_kernel(partial_ref, gain_ref, place_ref, out_ref, wide):
    devs, requests, width = partial_ref.shape
    tile = width // 8
    square = jnp.zeros((requests, 1), F32)
    for t in range(0, width, tile):
        total = partial_ref[0, :, t : t + tile].astype(F32)
        for d in range(1, devs):
            total += partial_ref[d, :, t : t + tile].astype(F32)
        attended = total.astype(BF16).astype(F32)
        wide[:, t : t + tile] = attended
        square += jnp.sum(attended * attended, axis=1, keepdims=True)
    factor = lax.rsqrt(square / width + 1e-06)
    for t in range(0, width, tile):
        normed = (wide[:, t : t + tile] * factor * gain_ref[:, t : t + tile]).astype(BF16)
        rows = jnp.dot(place_ref[...], normed, preferred_element_type=F32).astype(BF16)
        for e in range(out_ref.shape[0]):
            out_ref[e, :, t : t + tile] = rows[e * CAP : (e + 1) * CAP]


def dispatch_rows(partial, gain, place):
    _, requests, width = partial.shape
    slots = place.shape[0]
    return pl.pallas_call(
        dispatch_kernel,
        out_shape=jax.ShapeDtypeStruct((slots // CAP, CAP, width), BF16),
        in_specs=[pl.BlockSpec(memory_space=pltpu.VMEM)] * 3,
        out_specs=pl.BlockSpec(memory_space=pltpu.VMEM),
        scratch_shapes=[pltpu.VMEM((requests, width), F32)],
        compiler_params=pltpu.CompilerParams(vmem_limit_bytes=10 * 1024 * 1024),
        cost_estimate=pl.CostEstimate(
            flops=2 * slots * requests * width,
            bytes_accessed=2 * partial.size,
            transcendentals=0,
        ),
    )(partial, gain, place)


def mix_kernel(ring, weight_ref, rows_ref, out_ref):
    width = rows_ref.shape[2]
    slots = weight_ref.shape[1]
    experts = slots // CAP
    shards = rows_ref.shape[0] // experts
    for z in range(ring):
        rows = jnp.concatenate(
            [
                sum(rows_ref[e * shards + s].astype(F32) for s in range(z, shards, ring))
                for e in range(experts)
            ],
            axis=0,
        )
        out_ref[:, z * width : (z + 1) * width] = jnp.dot(
            weight_ref[...], rows, precision=lax.Precision.HIGHEST, preferred_element_type=F32
        ).astype(BF16)


def mix(weight, rows, ring):
    requests, slots = weight.shape
    width = rows.shape[2]
    return pl.pallas_call(
        functools.partial(mix_kernel, ring),
        out_shape=jax.ShapeDtypeStruct((requests, ring * width), BF16),
        in_specs=[pl.BlockSpec(memory_space=pltpu.VMEM)] * 2,
        out_specs=pl.BlockSpec(memory_space=pltpu.VMEM),
        compiler_params=pltpu.CompilerParams(vmem_limit_bytes=10 * 1024 * 1024),
        cost_estimate=pl.CostEstimate(
            flops=2 * requests * slots * ring * width,
            bytes_accessed=2 * rows.size,
            transcendentals=0,
        ),
    )(weight, rows)


def per_device(
    q_nope,
    q_rope,
    w_absorb_k,
    latent_cache,
    rope_keys,
    cache_lengths,
    w_absorb_v,
    w_out,
    norm_gain,
    routes,
    expert_probs,
    group_probs,
    w_gate,
    w_up,
    w_down,
):
    batch_rows = q_nope.shape[0]
    heads_local, nope_width, latent_width = w_absorb_k.shape
    rope_width = q_rope.shape[1] // heads_local
    model_width = w_out.shape[1]
    requests, _, cache_len = rope_keys.shape
    devs = lax.axis_size("dev")
    groups = lax.axis_size("grp")
    shards = devs // EXP_GRP
    experts = EXP_GRP * groups
    top_count = routes.shape[1]
    softmax_scale = float(nope_width + rope_width) ** (-0.5)

    ring = shards // 2
    z_up = [(i, i // ring * ring + (i + 1) % ring) for i in range(devs)]
    z_down = [(i, i // ring * ring + (i + ring - 1) % ring) for i in range(devs)]
    y_pair = [(i, i ^ ring) for i in range(devs)]

    units = w_down.shape[1]
    place = lax.axis_index("dev") % shards
    split = shards // ring
    half_width = model_width // shards
    layout = [(0, 0), (1, 0), (3, 0), (2, 0)]
    widths = [half_width * split] * ring
    down_out = column_blocks(w_down, layout, ring, widths)

    def relay(i):
        way = [(j, j // ring * ring + (j + layout[i][0]) % ring) for j in range(devs)]
        return lax.ppermute(down_out[i], "dev", way)

    query = absorb(q_nope, q_rope, w_absorb_k)
    query = query.reshape(devs, requests, query.shape[1])
    query = lax.all_to_all(query, "dev", split_axis=0, concat_axis=0, tiled=True)
    down = [down_out[0], relay(1), relay(2)]
    latent_out, w_out = attend(
        query, latent_cache, rope_keys, cache_lengths, w_out, heads_local, softmax_scale
    )
    head_latent = lax.all_to_all(latent_out, "dev", split_axis=0, concat_axis=0, tiled=True)
    partial = project(
        head_latent.reshape(batch_rows, heads_local * latent_width), w_absorb_v, w_out
    )
    partial, down, down_out = lax.optimization_barrier((partial, down, down_out))
    partial = lax.all_to_all(
        partial.reshape(devs, requests, model_width),
        "dev",
        split_axis=0,
        concat_axis=0,
        tiled=True,
    )
    partial, down_out = lax.optimization_barrier((partial, down_out))
    down = [*down, relay(3)]

    flat_routes = routes.reshape(requests * top_count)
    chosen = (flat_routes[:, None] == jnp.arange(experts)[None, :]).astype(jnp.int32)
    earlier = jnp.cumsum(chosen, axis=0) - chosen
    rank_in = jnp.sum(earlier * chosen, axis=1)
    slot_index = (flat_routes * CAP + rank_in).reshape(requests, top_count)
    slot_ids = jnp.arange(experts * CAP)
    placed = slot_index[None, :, :] == slot_ids[:, None, None]
    dispatch = jnp.any(placed, axis=2).astype(BF16)
    group_match = (routes // EXP_GRP)[:, :, None] == jnp.arange(groups)[None, None, :]
    group_weight = jnp.sum(jnp.where(group_match, group_probs[:, None, :], 0.0), axis=2)
    pair_weight = group_weight * expert_probs
    slot_weight = jnp.sum(jnp.where(placed, pair_weight[None], 0.0), axis=2).T
    outgoing = dispatch_rows(partial, norm_gain[None, :], dispatch)

    peers = [
        [g * devs + half * shards + p for g in range(groups) for half in range(EXP_GRP)]
        for p in range(shards)
    ]
    own = lax.all_to_all(
        outgoing,
        ("grp", "dev"),
        split_axis=0,
        concat_axis=0,
        tiled=True,
        axis_index_groups=peers,
    ).reshape(experts * CAP, model_width)

    own, down = lax.optimization_barrier((own, down))

    half_rows = own.shape[0] // 2
    lo, hi = slice(0, half_rows), slice(half_rows, None)

    def send(value, way):
        return lax.ppermute(value, "dev", way)

    below = send(own, z_up)
    above = send(own, z_down)
    beside = send(own, y_pair)
    first = expert_hidden([own, below, above, beside], w_gate, w_up)
    far_lo = send(below[lo], z_up)
    far_hi = send(above[hi], z_down)
    beside_below_lo = send(beside[lo], z_up)
    beside_above_hi = send(beside[hi], z_down)
    beside_below_hi = send(below[hi], y_pair)
    above_lo, beside_below_hi = lax.optimization_barrier((above[lo], beside_below_hi))
    beside_above_lo = send(above_lo, y_pair)
    second = expert_hidden(
        [far_lo, far_hi, beside_below_lo, beside_below_hi, beside_above_lo, beside_above_hi],
        w_gate,
        w_up,
    )
    beside_far_lo = send(beside_below_lo, z_up)
    beside_far_hi = send(beside_above_hi, z_down)
    beside_far_lo, beside_far_hi, first, second = lax.optimization_barrier(
        (beside_far_lo, beside_far_hi, first, second)
    )
    third = expert_hidden([beside_far_lo, beside_far_hi], w_gate, w_up)
    rows = own.shape[0]
    relative = jnp.concatenate([first, second, third], axis=0).reshape(shards, rows, units)
    order = jnp.array([0, 1, 4, 2, 3, 5, 7, 6], jnp.int32)
    position = jnp.arange(shards, dtype=jnp.int32)
    other = (position // ring) ^ (place // ring)
    steps = (place % ring - position % ring) % ring
    hidden = relative[order[other * ring + steps]].reshape(shards * rows, units)
    everyone = jnp.broadcast_to(hidden[None], (ring, shards * rows, units))
    rings = [[start + z for z in range(ring)] for start in range(0, devs, ring)]
    everyone = lax.all_to_all(
        everyone, "dev", split_axis=0, concat_axis=0, tiled=True, axis_index_groups=rings
    )
    result = expert_down(everyone, down, layout, groups, split)
    result = lax.all_to_all(result, ("grp", "dev"), split_axis=0, concat_axis=0, tiled=True)
    return mix(slot_weight, result, ring)


def solution(mesh):
    placed = (
        P("grp", "dev"),
        P("grp", "dev"),
        P("dev", None, None),
        P(("grp", "dev"), None, None),
        P(("grp", "dev"), None, None),
        P(("grp", "dev")),
        P("dev", None, None),
        P("dev", None),
        P(),
        P(("grp", "dev"), None),
        P(("grp", "dev"), None),
        P(("grp", "dev"), None),
        P(("grp", "dev"), None, None),
        P(("grp", "dev"), None, None),
        P(("grp", "dev"), None, None),
    )
    return jax.shard_map(
        per_device, mesh=mesh, in_specs=placed, out_specs=P(("grp", "dev"), None), check_vma=False
    )
```

```python
import functools

import jax
import jax.numpy as jnp
from jax import lax
from jax.experimental import pallas as pl
from jax.experimental.pallas import tpu as pltpu
from jax.sharding import PartitionSpec as P

EXP_GRP = 2
CAP = 4
LIMIT = 56 * 1024 * 1024
F32 = jnp.float32
BF16 = jnp.bfloat16


def hidden_kernel(count, *refs):
    row_refs = refs[:count]
    gate_ref, up_ref, out_ref, gate_sum, up_sum = refs[count:]
    step = pl.program_id(0)

    @pl.when(step == 0)
    def _():
        gate_sum[...] = jnp.zeros_like(gate_sum)
        up_sum[...] = jnp.zeros_like(up_sum)

    rows = jnp.concatenate([ref[...] for ref in row_refs], axis=0)
    gate_sum[...] += jnp.dot(rows, gate_ref[0], preferred_element_type=F32)
    up_sum[...] += jnp.dot(rows, up_ref[0], preferred_element_type=F32)

    @pl.when(step == pl.num_programs(0) - 1)
    def _():
        gate = gate_sum[...]
        out_ref[...] = (gate * jax.nn.sigmoid(gate) * up_sum[...]).astype(BF16)


def expert_hidden(blocks, w_gate, w_up, tile=1792):
    rows = sum(block.shape[0] for block in blocks)
    width, units = w_gate.shape[1:]
    return pl.pallas_call(
        functools.partial(hidden_kernel, len(blocks)),
        grid=(width // tile,),
        out_shape=jax.ShapeDtypeStruct((rows, units), BF16),
        in_specs=[pl.BlockSpec((block.shape[0], tile), lambda i: (0, i)) for block in blocks]
        + [pl.BlockSpec((1, tile, units), lambda i: (0, i, 0))] * 2,
        out_specs=pl.BlockSpec((rows, units), lambda i: (0, 0)),
        scratch_shapes=[pltpu.VMEM((rows, units), F32)] * 2,
        compiler_params=pltpu.CompilerParams(vmem_limit_bytes=14 * 1024 * 1024),
        cost_estimate=pl.CostEstimate(
            flops=4 * rows * width * units,
            bytes_accessed=2 * width * (2 * units + rows),
            transcendentals=rows * units,
        ),
    )(*blocks, w_gate, w_up)


def relay_kernel(layout, ring, weight_ref, *refs):
    count = len(layout)
    width = weight_ref.shape[2] // (2 * ring)
    place = lax.axis_index("dev") % ring
    out_refs, held, in_sems, out_sems = refs[:count], *refs[count:]
    arriving, leaving, offset = [], [], 0
    for k in range(count):
        size = out_refs[k].shape[1]
        part = held.at[:, pl.ds(offset, size)]
        block, half = layout[k]
        target = (place + block) % ring
        start = pl.multiple_of((2 * target + half) * width, 128)
        arriving.append(
            pltpu.make_async_copy(weight_ref.at[0, :, pl.ds(start, size)], part, in_sems.at[k])
        )
        leaving.append(pltpu.make_async_copy(part, out_refs[k], out_sems.at[k]))
        offset += size
    for copy in arriving:
        copy.start()
    for k in range(count):
        arriving[k].wait()
        leaving[k].start()
    for copy in leaving:
        copy.wait()


def column_blocks(weight, layout, ring, widths):
    _, rows, columns = weight.shape
    count = len(widths)
    return pl.pallas_call(
        functools.partial(relay_kernel, layout, ring),
        out_shape=[jax.ShapeDtypeStruct((rows, width), weight.dtype) for width in widths],
        in_specs=[pl.BlockSpec(memory_space=pltpu.HBM)],
        out_specs=[pl.BlockSpec(memory_space=pltpu.HBM)] * count,
        scratch_shapes=[
            pltpu.VMEM((rows, columns), weight.dtype),
            pltpu.SemaphoreType.DMA((count,)),
            pltpu.SemaphoreType.DMA((count,)),
        ],
        compiler_params=pltpu.CompilerParams(vmem_limit_bytes=LIMIT),
        cost_estimate=pl.CostEstimate(
            flops=0, bytes_accessed=4 * rows * columns, transcendentals=0
        ),
    )(weight)


def down_kernel(groups, layout, hidden_ref, *refs):
    ring, total, units = hidden_ref.shape
    count = len(layout)
    down_refs, out_ref, hidden, down, hidden_sems, sems = refs[:count], *refs[count:]
    halves = sems.shape[0]
    width = out_ref.shape[2] // halves
    place = lax.axis_index("dev") % ring
    hidden_copies = [
        pltpu.make_async_copy(
            hidden_ref.at[(place + ring - k) % ring],
            hidden.at[:, pl.ds(k * units, units)],
            hidden_sems.at[k],
        )
        for k in range(ring)
    ]
    down_copies = [[] for _ in range(halves)]
    for ref, (k, first) in zip(down_refs, layout):
        for half in range(first, first + ref.shape[1] // width):
            down_copies[half].append(
                pltpu.make_async_copy(
                    ref.at[:, pl.ds((half - first) * width, width)],
                    down.at[pl.ds(k * units, units), pl.ds(half * width, width)],
                    sems.at[half, k],
                )
            )
    for copy in hidden_copies + [copy for part in down_copies for copy in part]:
        copy.start()
    for copy in hidden_copies:
        copy.wait()
    peers = groups * EXP_GRP
    rows = peers * CAP
    places = total // rows
    for half in range(halves):
        for copy in down_copies[half]:
            copy.wait()
        columns = slice(half * width, (half + 1) * width)
        value = jnp.dot(hidden[...], down[:, columns], preferred_element_type=F32).astype(BF16)
        for place in range(places):
            for peer in range(peers):
                row = place * rows + peer * CAP
                out_ref[peer * places + place, :, columns] = value[row : row + CAP]


def expert_down(hidden, down, layout, groups, halves):
    ring, rows, units = hidden.shape
    width = sum(piece.shape[1] for piece in down) // ring
    return pl.pallas_call(
        functools.partial(down_kernel, groups, layout),
        out_shape=jax.ShapeDtypeStruct((rows // CAP, CAP, width), BF16),
        in_specs=[pl.BlockSpec(memory_space=pltpu.VMEM)]
        + [pl.BlockSpec(memory_space=pltpu.HBM)] * len(down),
        out_specs=pl.BlockSpec(memory_space=pltpu.VMEM),
        scratch_shapes=[
            pltpu.VMEM((rows, ring * units), BF16),
            pltpu.VMEM((ring * units, width), BF16),
            pltpu.SemaphoreType.DMA((ring,)),
            pltpu.SemaphoreType.DMA((halves, ring)),
        ],
        compiler_params=pltpu.CompilerParams(vmem_limit_bytes=24 * 1024 * 1024),
        cost_estimate=pl.CostEstimate(
            flops=2 * ring * rows * units * width,
            bytes_accessed=2 * (ring * units * (rows + width) + rows * width),
            transcendentals=0,
        ),
    )(hidden, *down)


def absorb_kernel(nope_ref, rope_ref, weight_ref, out_ref, nope, rope, weight, sems):
    copies = [
        pltpu.make_async_copy(source, target, sems.at[i])
        for i, (source, target) in enumerate(
            ((nope_ref, nope), (weight_ref, weight), (rope_ref, rope))
        )
    ]
    for copy in copies:
        copy.start()
    copies[0].wait()
    copies[1].wait()
    heads, width, latent = weight.shape
    for h in range(heads):
        out_ref[:, h * latent : (h + 1) * latent] = jnp.dot(
            nope[:, h * width : (h + 1) * width], weight[h], preferred_element_type=F32
        ).astype(BF16)
    copies[2].wait()
    out_ref[:, heads * latent :] = rope[...]


def absorb(q_nope, q_rope, w_absorb_k):
    rows = q_nope.shape[0]
    heads, width, latent = w_absorb_k.shape
    columns = heads * latent + q_rope.shape[1]
    return pl.pallas_call(
        absorb_kernel,
        out_shape=jax.ShapeDtypeStruct((rows, columns), BF16),
        in_specs=[pl.BlockSpec(memory_space=pltpu.HBM)] * 3,
        out_specs=pl.BlockSpec(memory_space=pltpu.VMEM),
        scratch_shapes=[
            pltpu.VMEM(q_nope.shape, BF16),
            pltpu.VMEM(q_rope.shape, BF16),
            pltpu.VMEM(w_absorb_k.shape, BF16),
            pltpu.SemaphoreType.DMA((3,)),
        ],
        compiler_params=pltpu.CompilerParams(vmem_limit_bytes=LIMIT),
        cost_estimate=pl.CostEstimate(
            flops=2 * rows * heads * width * latent,
            bytes_accessed=2 * (rows * columns + heads * width * latent),
            transcendentals=0,
        ),
    )(q_nope, q_rope, w_absorb_k)


def attend_kernel(heads, scale, length_ref, query_ref, cache_hbm, keys_hbm, weight_hbm, *refs):
    out_ref, weight_ref, cache_ref, keys_ref, queries, values, sems = refs
    devs, requests, columns = query_ref.shape
    rope = keys_ref.shape[1]
    latent = cache_ref.shape[2]
    rows = devs * requests
    keys_copy = pltpu.make_async_copy(keys_hbm, keys_ref, sems.at[requests])
    cache_copies = [
        pltpu.make_async_copy(cache_hbm.at[r], cache_ref.at[r], sems.at[r])
        for r in range(requests)
    ]
    keys_copy.start()
    for copy in cache_copies:
        copy.start()
    weight_copy = pltpu.make_async_copy(weight_hbm, weight_ref, sems.at[requests + 1])
    weight_copy.start()
    row = lax.broadcasted_iota(jnp.int32, (rows, rows), 0)
    column = lax.broadcasted_iota(jnp.int32, (rows, rows), 1)
    by_request = (column == row % devs * requests + row // devs).astype(BF16)
    by_device = (column == row % requests * devs + row // requests).astype(BF16)
    queries[...] = jnp.dot(
        by_request, query_ref[...].reshape(rows, columns), preferred_element_type=F32
    ).astype(BF16)
    split = heads * latent
    keys_copy.wait()
    group = 4
    for first in range(0, requests, group):
        members = range(first, first + group)
        for r in members:
            cache_copies[r].wait()
        scores = []
        for r in members:
            mine = slice(r * devs, (r + 1) * devs)
            latents = jnp.concatenate(
                [queries[mine, h * latent : (h + 1) * latent] for h in range(heads)], axis=0
            )
            ropes = jnp.concatenate(
                [queries[mine, split + h * rope : split + (h + 1) * rope] for h in range(heads)],
                axis=0,
            )
            scores.append(
                lax.dot_general(
                    latents, cache_ref[r], (((1,), (1,)), ((), ())), preferred_element_type=F32
                )
                + jnp.dot(ropes, keys_ref[r], preferred_element_type=F32)
            )
        probs = []
        for r, score in zip(members, scores):
            live = lax.broadcasted_iota(jnp.int32, score.shape, 1) < length_ref[r]
            score = jnp.where(live, score * scale, -jnp.inf)
            exponent = jnp.exp(score - jnp.max(score, axis=1, keepdims=True))
            probs.append((exponent / jnp.sum(exponent, axis=1, keepdims=True)).astype(BF16))
        for r, prob in zip(members, probs):
            value = jnp.dot(prob, cache_ref[r], preferred_element_type=F32).astype(BF16)
            for h in range(heads):
                values[r * devs : (r + 1) * devs, h * latent : (h + 1) * latent] = value[
                    h * devs : (h + 1) * devs
                ]
    out_ref[...] = (
        jnp.dot(by_device, values[...], preferred_element_type=F32)
        .astype(BF16)
        .reshape(out_ref.shape)
    )
    weight_copy.wait()


def attend(query, latent_cache, rope_keys, lengths, w_out, heads, scale):
    devs, requests, columns = query.shape
    _, rope, positions = rope_keys.shape
    latent = latent_cache.shape[2]
    rows = heads * devs
    return pl.pallas_call(
        functools.partial(attend_kernel, heads, scale),
        out_shape=[
            jax.ShapeDtypeStruct((devs, requests, heads * latent), BF16),
            jax.ShapeDtypeStruct(w_out.shape, BF16),
        ],
        in_specs=[
            pl.BlockSpec(memory_space=pltpu.SMEM),
            pl.BlockSpec(memory_space=pltpu.VMEM),
            pl.BlockSpec(memory_space=pltpu.HBM),
            pl.BlockSpec(memory_space=pltpu.HBM),
            pl.BlockSpec(memory_space=pltpu.HBM),
        ],
        out_specs=[pl.BlockSpec(memory_space=pltpu.VMEM)] * 2,
        scratch_shapes=[
            pltpu.VMEM(latent_cache.shape, BF16),
            pltpu.VMEM(rope_keys.shape, BF16),
            pltpu.VMEM((devs * requests, columns), BF16),
            pltpu.VMEM((devs * requests, heads * latent), BF16),
            pltpu.SemaphoreType.DMA((requests + 2,)),
        ],
        compiler_params=pltpu.CompilerParams(vmem_limit_bytes=28 * 1024 * 1024),
        cost_estimate=pl.CostEstimate(
            flops=2 * requests * rows * positions * (2 * latent + rope),
            bytes_accessed=2 * requests * positions * (latent + rope),
            transcendentals=requests * rows * positions,
        ),
    )(lengths, query, latent_cache, rope_keys, w_out)


def project_kernel(latent_ref, absorb_ref, weight_ref, out_ref):
    heads, latent, _ = absorb_ref.shape
    values = jnp.concatenate(
        [
            jnp.dot(
                latent_ref[:, h * latent : (h + 1) * latent],
                absorb_ref[h],
                preferred_element_type=F32,
            ).astype(BF16)
            for h in range(heads)
        ],
        axis=1,
    )
    tile = 1024
    for t in range(0, weight_ref.shape[1], tile):
        out_ref[:, t : t + tile] = jnp.dot(
            values, weight_ref[:, t : t + tile], preferred_element_type=F32
        ).astype(BF16)


def project(head_latent, w_absorb_v, w_out):
    rows = head_latent.shape[0]
    depth, columns = w_out.shape
    return pl.pallas_call(
        project_kernel,
        out_shape=jax.ShapeDtypeStruct((rows, columns), BF16),
        in_specs=[pl.BlockSpec(memory_space=pltpu.VMEM)] * 3,
        out_specs=pl.BlockSpec(memory_space=pltpu.VMEM),
        compiler_params=pltpu.CompilerParams(vmem_limit_bytes=24 * 1024 * 1024),
        cost_estimate=pl.CostEstimate(
            flops=2 * rows * (depth * columns + w_absorb_v.size),
            bytes_accessed=2 * (depth * columns + rows * columns),
            transcendentals=0,
        ),
    )(head_latent, w_absorb_v, w_out)


def dispatch_kernel(partial_ref, gain_ref, place_ref, out_ref, wide):
    devs, requests, width = partial_ref.shape
    tile = width // 8
    square = jnp.zeros((requests, 1), F32)
    for t in range(0, width, tile):
        total = partial_ref[0, :, t : t + tile].astype(F32)
        for d in range(1, devs):
            total += partial_ref[d, :, t : t + tile].astype(F32)
        attended = total.astype(BF16).astype(F32)
        wide[:, t : t + tile] = attended
        square += jnp.sum(attended * attended, axis=1, keepdims=True)
    factor = lax.rsqrt(square / width + 1e-06)
    for t in range(0, width, tile):
        normed = (wide[:, t : t + tile] * factor * gain_ref[:, t : t + tile]).astype(BF16)
        rows = jnp.dot(place_ref[...], normed, preferred_element_type=F32).astype(BF16)
        for e in range(out_ref.shape[0]):
            out_ref[e, :, t : t + tile] = rows[e * CAP : (e + 1) * CAP]


def dispatch_rows(partial, gain, place):
    _, requests, width = partial.shape
    slots = place.shape[0]
    return pl.pallas_call(
        dispatch_kernel,
        out_shape=jax.ShapeDtypeStruct((slots // CAP, CAP, width), BF16),
        in_specs=[pl.BlockSpec(memory_space=pltpu.VMEM)] * 3,
        out_specs=pl.BlockSpec(memory_space=pltpu.VMEM),
        scratch_shapes=[pltpu.VMEM((requests, width), F32)],
        compiler_params=pltpu.CompilerParams(vmem_limit_bytes=10 * 1024 * 1024),
        cost_estimate=pl.CostEstimate(
            flops=2 * slots * requests * width,
            bytes_accessed=2 * partial.size,
            transcendentals=0,
        ),
    )(partial, gain, place)


def mix_kernel(ring, weight_ref, rows_ref, out_ref):
    width = rows_ref.shape[2]
    slots = weight_ref.shape[1]
    experts = slots // CAP
    shards = rows_ref.shape[0] // experts
    for z in range(ring):
        rows = jnp.concatenate(
            [
                sum(rows_ref[e * shards + s].astype(F32) for s in range(z, shards, ring))
                for e in range(experts)
            ],
            axis=0,
        )
        out_ref[:, z * width : (z + 1) * width] = jnp.dot(
            weight_ref[...], rows, precision=lax.Precision.HIGHEST, preferred_element_type=F32
        ).astype(BF16)


def mix(weight, rows, ring):
    requests, slots = weight.shape
    width = rows.shape[2]
    return pl.pallas_call(
        functools.partial(mix_kernel, ring),
        out_shape=jax.ShapeDtypeStruct((requests, ring * width), BF16),
        in_specs=[pl.BlockSpec(memory_space=pltpu.VMEM)] * 2,
        out_specs=pl.BlockSpec(memory_space=pltpu.VMEM),
        compiler_params=pltpu.CompilerParams(vmem_limit_bytes=10 * 1024 * 1024),
        cost_estimate=pl.CostEstimate(
            flops=2 * requests * slots * ring * width,
            bytes_accessed=2 * rows.size,
            transcendentals=0,
        ),
    )(weight, rows)


def per_device(
    q_nope,
    q_rope,
    w_absorb_k,
    latent_cache,
    rope_keys,
    cache_lengths,
    w_absorb_v,
    w_out,
    norm_gain,
    routes,
    expert_probs,
    group_probs,
    w_gate,
    w_up,
    w_down,
):
    batch_rows = q_nope.shape[0]
    heads_local, nope_width, latent_width = w_absorb_k.shape
    rope_width = q_rope.shape[1] // heads_local
    model_width = w_out.shape[1]
    requests, _, cache_len = rope_keys.shape
    devs = lax.axis_size("dev")
    groups = lax.axis_size("grp")
    shards = devs // EXP_GRP
    experts = EXP_GRP * groups
    top_count = routes.shape[1]
    softmax_scale = float(nope_width + rope_width) ** (-0.5)

    ring = shards // 2
    z_up = [(i, i // ring * ring + (i + 1) % ring) for i in range(devs)]
    z_down = [(i, i // ring * ring + (i + ring - 1) % ring) for i in range(devs)]
    y_pair = [(i, i ^ ring) for i in range(devs)]

    units = w_down.shape[1]
    place = lax.axis_index("dev") % shards
    split = shards // ring
    half_width = model_width // shards
    layout = [(0, 0), (1, 0), (3, 0), (2, 0)]
    widths = [half_width * split] * ring
    down_out = column_blocks(w_down, layout, ring, widths)

    def relay(i):
        way = [(j, j // ring * ring + (j + layout[i][0]) % ring) for j in range(devs)]
        return lax.ppermute(down_out[i], "dev", way)

    query = absorb(q_nope, q_rope, w_absorb_k)
    query = query.reshape(devs, requests, query.shape[1])
    query = lax.all_to_all(query, "dev", split_axis=0, concat_axis=0, tiled=True)
    down = [down_out[0], relay(1), relay(2)]
    latent_out, w_out = attend(
        query, latent_cache, rope_keys, cache_lengths, w_out, heads_local, softmax_scale
    )
    head_latent = lax.all_to_all(latent_out, "dev", split_axis=0, concat_axis=0, tiled=True)
    partial = project(
        head_latent.reshape(batch_rows, heads_local * latent_width), w_absorb_v, w_out
    )
    partial, down, down_out = lax.optimization_barrier((partial, down, down_out))
    partial = lax.all_to_all(
        partial.reshape(devs, requests, model_width),
        "dev",
        split_axis=0,
        concat_axis=0,
        tiled=True,
    )
    flat_routes = routes.reshape(requests * top_count)
    chosen = (flat_routes[:, None] == jnp.arange(experts)[None, :]).astype(jnp.int32)
    earlier = jnp.cumsum(chosen, axis=0) - chosen
    rank_in = jnp.sum(earlier * chosen, axis=1)
    slot_index = (flat_routes * CAP + rank_in).reshape(requests, top_count)
    slot_ids = jnp.arange(experts * CAP)
    placed = slot_index[None, :, :] == slot_ids[:, None, None]
    dispatch = jnp.any(placed, axis=2).astype(BF16)
    group_match = (routes // EXP_GRP)[:, :, None] == jnp.arange(groups)[None, None, :]
    group_weight = jnp.sum(jnp.where(group_match, group_probs[:, None, :], 0.0), axis=2)
    pair_weight = group_weight * expert_probs
    slot_weight = jnp.sum(jnp.where(placed, pair_weight[None], 0.0), axis=2).T

    partial, down_out, dispatch, slot_weight = lax.optimization_barrier(
        (partial, down_out, dispatch, slot_weight)
    )
    down = [*down, relay(3)]

    outgoing = dispatch_rows(partial, norm_gain[None, :], dispatch)

    peers = [
        [g * devs + half * shards + p for g in range(groups) for half in range(EXP_GRP)]
        for p in range(shards)
    ]
    own = lax.all_to_all(
        outgoing,
        ("grp", "dev"),
        split_axis=0,
        concat_axis=0,
        tiled=True,
        axis_index_groups=peers,
    ).reshape(experts * CAP, model_width)

    own, down = lax.optimization_barrier((own, down))

    half_rows = own.shape[0] // 2
    lo, hi = slice(0, half_rows), slice(half_rows, None)

    def send(value, way):
        return lax.ppermute(value, "dev", way)

    below_lo = send(own[lo], z_up)
    above_hi = send(own[hi], z_down)
    beside = send(own, y_pair)
    below_hi = send(own[hi], z_up)
    above_lo = send(own[lo], z_down)
    first = expert_hidden([own, below_lo, below_hi, above_lo, above_hi, beside], w_gate, w_up)
    far_lo = send(below_lo, z_up)
    far_hi = send(above_hi, z_down)
    beside_below_lo = send(beside[lo], z_up)
    beside_above_hi = send(beside[hi], z_down)
    beside_below_hi = send(below_hi, y_pair)
    above_lo, beside_below_hi = lax.optimization_barrier((above_lo, beside_below_hi))
    beside_above_lo = send(above_lo, y_pair)
    second = expert_hidden(
        [far_lo, far_hi, beside_below_lo, beside_below_hi, beside_above_lo, beside_above_hi],
        w_gate,
        w_up,
    )
    beside_far_lo = send(beside_below_lo, z_up)
    beside_far_hi = send(beside_above_hi, z_down)
    beside_far_lo, beside_far_hi, first, second = lax.optimization_barrier(
        (beside_far_lo, beside_far_hi, first, second)
    )
    third = expert_hidden([beside_far_lo, beside_far_hi], w_gate, w_up)
    rows = own.shape[0]
    relative = jnp.concatenate([first, second, third], axis=0).reshape(shards, rows, units)
    order = jnp.array([0, 1, 4, 2, 3, 5, 7, 6], jnp.int32)
    position = jnp.arange(shards, dtype=jnp.int32)
    other = (position // ring) ^ (place // ring)
    steps = (place % ring - position % ring) % ring
    hidden = relative[order[other * ring + steps]].reshape(shards * rows, units)
    everyone = jnp.broadcast_to(hidden[None], (ring, shards * rows, units))
    rings = [[start + z for z in range(ring)] for start in range(0, devs, ring)]
    everyone = lax.all_to_all(
        everyone, "dev", split_axis=0, concat_axis=0, tiled=True, axis_index_groups=rings
    )
    result = expert_down(everyone, down, layout, groups, split)
    result = lax.all_to_all(result, ("grp", "dev"), split_axis=0, concat_axis=0, tiled=True)
    return mix(slot_weight, result, ring)


def solution(mesh):
    placed = (
        P("grp", "dev"),
        P("grp", "dev"),
        P("dev", None, None),
        P(("grp", "dev"), None, None),
        P(("grp", "dev"), None, None),
        P(("grp", "dev")),
        P("dev", None, None),
        P("dev", None),
        P(),
        P(("grp", "dev"), None),
        P(("grp", "dev"), None),
        P(("grp", "dev"), None),
        P(("grp", "dev"), None, None),
        P(("grp", "dev"), None, None),
        P(("grp", "dev"), None, None),
    )
    return jax.shard_map(
        per_device, mesh=mesh, in_specs=placed, out_specs=P(("grp", "dev"), None), check_vma=False
    )
```

```python
import functools

import jax
import jax.numpy as jnp
from jax import lax
from jax.experimental import pallas as pl
from jax.experimental.pallas import tpu as pltpu
from jax.sharding import PartitionSpec as P

EXP_GRP = 2
CAP = 4
LIMIT = 56 * 1024 * 1024
F32 = jnp.float32
BF16 = jnp.bfloat16


def hidden_kernel(count, *refs):
    row_refs = refs[:count]
    gate_ref, up_ref, out_ref, gate_sum, up_sum = refs[count:]
    step = pl.program_id(0)

    @pl.when(step == 0)
    def _():
        gate_sum[...] = jnp.zeros_like(gate_sum)
        up_sum[...] = jnp.zeros_like(up_sum)

    rows = jnp.concatenate([ref[...] for ref in row_refs], axis=0)
    gate_sum[...] += jnp.dot(rows, gate_ref[0], preferred_element_type=F32)
    up_sum[...] += jnp.dot(rows, up_ref[0], preferred_element_type=F32)

    @pl.when(step == pl.num_programs(0) - 1)
    def _():
        gate = gate_sum[...]
        out_ref[...] = (gate * jax.nn.sigmoid(gate) * up_sum[...]).astype(BF16)


def expert_hidden(blocks, w_gate, w_up, tile=1792):
    rows = sum(block.shape[0] for block in blocks)
    width, units = w_gate.shape[1:]
    return pl.pallas_call(
        functools.partial(hidden_kernel, len(blocks)),
        grid=(width // tile,),
        out_shape=jax.ShapeDtypeStruct((rows, units), BF16),
        in_specs=[pl.BlockSpec((block.shape[0], tile), lambda i: (0, i)) for block in blocks]
        + [pl.BlockSpec((1, tile, units), lambda i: (0, i, 0))] * 2,
        out_specs=pl.BlockSpec((rows, units), lambda i: (0, 0)),
        scratch_shapes=[pltpu.VMEM((rows, units), F32)] * 2,
        compiler_params=pltpu.CompilerParams(vmem_limit_bytes=14 * 1024 * 1024),
        cost_estimate=pl.CostEstimate(
            flops=4 * rows * width * units,
            bytes_accessed=2 * width * (2 * units + rows),
            transcendentals=rows * units,
        ),
    )(*blocks, w_gate, w_up)


def relay_kernel(layout, ring, weight_ref, *refs):
    count = len(layout)
    width = weight_ref.shape[2] // (2 * ring)
    place = lax.axis_index("dev") % ring
    out_refs, held, in_sems, out_sems = refs[:count], *refs[count:]
    arriving, leaving, offset = [], [], 0
    for k in range(count):
        size = out_refs[k].shape[1]
        part = held.at[:, pl.ds(offset, size)]
        block, half = layout[k]
        target = (place + block) % ring
        start = pl.multiple_of((2 * target + half) * width, 128)
        arriving.append(
            pltpu.make_async_copy(weight_ref.at[0, :, pl.ds(start, size)], part, in_sems.at[k])
        )
        leaving.append(pltpu.make_async_copy(part, out_refs[k], out_sems.at[k]))
        offset += size
    for copy in arriving:
        copy.start()
    for k in range(count):
        arriving[k].wait()
        leaving[k].start()
    for copy in leaving:
        copy.wait()


def column_blocks(weight, layout, ring, widths):
    _, rows, columns = weight.shape
    count = len(widths)
    return pl.pallas_call(
        functools.partial(relay_kernel, layout, ring),
        out_shape=[jax.ShapeDtypeStruct((rows, width), weight.dtype) for width in widths],
        in_specs=[pl.BlockSpec(memory_space=pltpu.HBM)],
        out_specs=[pl.BlockSpec(memory_space=pltpu.HBM)] * count,
        scratch_shapes=[
            pltpu.VMEM((rows, columns), weight.dtype),
            pltpu.SemaphoreType.DMA((count,)),
            pltpu.SemaphoreType.DMA((count,)),
        ],
        compiler_params=pltpu.CompilerParams(vmem_limit_bytes=LIMIT),
        cost_estimate=pl.CostEstimate(
            flops=0, bytes_accessed=4 * rows * columns, transcendentals=0
        ),
    )(weight)


def down_kernel(groups, layout, hidden_ref, *refs):
    ring, total, units = hidden_ref.shape
    count = len(layout)
    down_refs, out_ref, hidden, down, hidden_sems, sems = refs[:count], *refs[count:]
    halves = sems.shape[0]
    width = out_ref.shape[2] // halves
    place = lax.axis_index("dev") % ring
    hidden_copies = [
        pltpu.make_async_copy(
            hidden_ref.at[(place + ring - k) % ring],
            hidden.at[:, pl.ds(k * units, units)],
            hidden_sems.at[k],
        )
        for k in range(ring)
    ]
    down_copies = [[] for _ in range(halves)]
    for ref, (k, first) in zip(down_refs, layout):
        for half in range(first, first + ref.shape[1] // width):
            down_copies[half].append(
                pltpu.make_async_copy(
                    ref.at[:, pl.ds((half - first) * width, width)],
                    down.at[pl.ds(k * units, units), pl.ds(half * width, width)],
                    sems.at[half, k],
                )
            )
    for copy in hidden_copies + [copy for part in down_copies for copy in part]:
        copy.start()
    for copy in hidden_copies:
        copy.wait()
    peers = groups * EXP_GRP
    rows = peers * CAP
    places = total // rows
    for half in range(halves):
        for copy in down_copies[half]:
            copy.wait()
        columns = slice(half * width, (half + 1) * width)
        value = jnp.dot(hidden[...], down[:, columns], preferred_element_type=F32).astype(BF16)
        for place in range(places):
            for peer in range(peers):
                row = place * rows + peer * CAP
                out_ref[peer * places + place, :, columns] = value[row : row + CAP]


def expert_down(hidden, down, layout, groups, halves):
    ring, rows, units = hidden.shape
    width = sum(piece.shape[1] for piece in down) // ring
    return pl.pallas_call(
        functools.partial(down_kernel, groups, layout),
        out_shape=jax.ShapeDtypeStruct((rows // CAP, CAP, width), BF16),
        in_specs=[pl.BlockSpec(memory_space=pltpu.VMEM)]
        + [pl.BlockSpec(memory_space=pltpu.HBM)] * len(down),
        out_specs=pl.BlockSpec(memory_space=pltpu.VMEM),
        scratch_shapes=[
            pltpu.VMEM((rows, ring * units), BF16),
            pltpu.VMEM((ring * units, width), BF16),
            pltpu.SemaphoreType.DMA((ring,)),
            pltpu.SemaphoreType.DMA((halves, ring)),
        ],
        compiler_params=pltpu.CompilerParams(vmem_limit_bytes=24 * 1024 * 1024),
        cost_estimate=pl.CostEstimate(
            flops=2 * ring * rows * units * width,
            bytes_accessed=2 * (ring * units * (rows + width) + rows * width),
            transcendentals=0,
        ),
    )(hidden, *down)


def absorb_kernel(nope_ref, rope_ref, weight_ref, out_ref, nope, rope, weight, sems):
    copies = [
        pltpu.make_async_copy(source, target, sems.at[i])
        for i, (source, target) in enumerate(
            ((nope_ref, nope), (weight_ref, weight), (rope_ref, rope))
        )
    ]
    for copy in copies:
        copy.start()
    copies[0].wait()
    copies[1].wait()
    heads, width, latent = weight.shape
    for h in range(heads):
        out_ref[:, h * latent : (h + 1) * latent] = jnp.dot(
            nope[:, h * width : (h + 1) * width], weight[h], preferred_element_type=F32
        ).astype(BF16)
    copies[2].wait()
    out_ref[:, heads * latent :] = rope[...]


def absorb(q_nope, q_rope, w_absorb_k):
    rows = q_nope.shape[0]
    heads, width, latent = w_absorb_k.shape
    columns = heads * latent + q_rope.shape[1]
    return pl.pallas_call(
        absorb_kernel,
        out_shape=jax.ShapeDtypeStruct((rows, columns), BF16),
        in_specs=[pl.BlockSpec(memory_space=pltpu.HBM)] * 3,
        out_specs=pl.BlockSpec(memory_space=pltpu.VMEM),
        scratch_shapes=[
            pltpu.VMEM(q_nope.shape, BF16),
            pltpu.VMEM(q_rope.shape, BF16),
            pltpu.VMEM(w_absorb_k.shape, BF16),
            pltpu.SemaphoreType.DMA((3,)),
        ],
        compiler_params=pltpu.CompilerParams(vmem_limit_bytes=LIMIT),
        cost_estimate=pl.CostEstimate(
            flops=2 * rows * heads * width * latent,
            bytes_accessed=2 * (rows * columns + heads * width * latent),
            transcendentals=0,
        ),
    )(q_nope, q_rope, w_absorb_k)


def attend_kernel(heads, scale, length_ref, query_ref, cache_hbm, keys_hbm, weight_hbm, *refs):
    out_ref, weight_ref, cache_ref, keys_ref, queries, values, sems = refs
    devs, requests, columns = query_ref.shape
    rope = keys_ref.shape[1]
    latent = cache_ref.shape[2]
    rows = devs * requests
    keys_copy = pltpu.make_async_copy(keys_hbm, keys_ref, sems.at[requests])
    cache_copies = [
        pltpu.make_async_copy(cache_hbm.at[r], cache_ref.at[r], sems.at[r])
        for r in range(requests)
    ]
    keys_copy.start()
    for copy in cache_copies:
        copy.start()
    weight_copy = pltpu.make_async_copy(weight_hbm, weight_ref, sems.at[requests + 1])
    weight_copy.start()
    row = lax.broadcasted_iota(jnp.int32, (rows, rows), 0)
    column = lax.broadcasted_iota(jnp.int32, (rows, rows), 1)
    by_request = (column == row % devs * requests + row // devs).astype(BF16)
    by_device = (column == row % requests * devs + row // requests).astype(BF16)
    queries[...] = jnp.dot(
        by_request, query_ref[...].reshape(rows, columns), preferred_element_type=F32
    ).astype(BF16)
    split = heads * latent
    keys_copy.wait()
    group = 4
    for first in range(0, requests, group):
        members = range(first, first + group)
        for r in members:
            cache_copies[r].wait()
        scores = []
        for r in members:
            mine = slice(r * devs, (r + 1) * devs)
            latents = jnp.concatenate(
                [queries[mine, h * latent : (h + 1) * latent] for h in range(heads)], axis=0
            )
            ropes = jnp.concatenate(
                [queries[mine, split + h * rope : split + (h + 1) * rope] for h in range(heads)],
                axis=0,
            )
            scores.append(
                lax.dot_general(
                    latents, cache_ref[r], (((1,), (1,)), ((), ())), preferred_element_type=F32
                )
                + jnp.dot(ropes, keys_ref[r], preferred_element_type=F32)
            )
        probs = []
        for r, score in zip(members, scores):
            live = lax.broadcasted_iota(jnp.int32, score.shape, 1) < length_ref[r]
            score = jnp.where(live, score * scale, -jnp.inf)
            exponent = jnp.exp(score - jnp.max(score, axis=1, keepdims=True))
            probs.append((exponent / jnp.sum(exponent, axis=1, keepdims=True)).astype(BF16))
        for r, prob in zip(members, probs):
            value = jnp.dot(prob, cache_ref[r], preferred_element_type=F32).astype(BF16)
            for h in range(heads):
                values[r * devs : (r + 1) * devs, h * latent : (h + 1) * latent] = value[
                    h * devs : (h + 1) * devs
                ]
    out_ref[...] = (
        jnp.dot(by_device, values[...], preferred_element_type=F32)
        .astype(BF16)
        .reshape(out_ref.shape)
    )
    weight_copy.wait()


def attend(query, latent_cache, rope_keys, lengths, w_out, heads, scale):
    devs, requests, columns = query.shape
    _, rope, positions = rope_keys.shape
    latent = latent_cache.shape[2]
    rows = heads * devs
    return pl.pallas_call(
        functools.partial(attend_kernel, heads, scale),
        out_shape=[
            jax.ShapeDtypeStruct((devs, requests, heads * latent), BF16),
            jax.ShapeDtypeStruct(w_out.shape, BF16),
        ],
        in_specs=[
            pl.BlockSpec(memory_space=pltpu.SMEM),
            pl.BlockSpec(memory_space=pltpu.VMEM),
            pl.BlockSpec(memory_space=pltpu.HBM),
            pl.BlockSpec(memory_space=pltpu.HBM),
            pl.BlockSpec(memory_space=pltpu.HBM),
        ],
        out_specs=[pl.BlockSpec(memory_space=pltpu.VMEM)] * 2,
        scratch_shapes=[
            pltpu.VMEM(latent_cache.shape, BF16),
            pltpu.VMEM(rope_keys.shape, BF16),
            pltpu.VMEM((devs * requests, columns), BF16),
            pltpu.VMEM((devs * requests, heads * latent), BF16),
            pltpu.SemaphoreType.DMA((requests + 2,)),
        ],
        compiler_params=pltpu.CompilerParams(vmem_limit_bytes=41 * 1024 * 1024),
        cost_estimate=pl.CostEstimate(
            flops=2 * requests * rows * positions * (2 * latent + rope),
            bytes_accessed=2 * requests * positions * (latent + rope),
            transcendentals=requests * rows * positions,
        ),
    )(lengths, query, latent_cache, rope_keys, w_out)


def project_kernel(latent_ref, absorb_ref, weight_ref, out_ref):
    heads, latent, _ = absorb_ref.shape
    values = jnp.concatenate(
        [
            jnp.dot(
                latent_ref[:, h * latent : (h + 1) * latent],
                absorb_ref[h],
                preferred_element_type=F32,
            ).astype(BF16)
            for h in range(heads)
        ],
        axis=1,
    )
    tile = 1024
    for t in range(0, weight_ref.shape[1], tile):
        out_ref[:, t : t + tile] = jnp.dot(
            values, weight_ref[:, t : t + tile], preferred_element_type=F32
        ).astype(BF16)


def project(head_latent, w_absorb_v, w_out):
    rows = head_latent.shape[0]
    depth, columns = w_out.shape
    return pl.pallas_call(
        project_kernel,
        out_shape=jax.ShapeDtypeStruct((rows, columns), BF16),
        in_specs=[pl.BlockSpec(memory_space=pltpu.VMEM)] * 3,
        out_specs=pl.BlockSpec(memory_space=pltpu.VMEM),
        compiler_params=pltpu.CompilerParams(vmem_limit_bytes=24 * 1024 * 1024),
        cost_estimate=pl.CostEstimate(
            flops=2 * rows * (depth * columns + w_absorb_v.size),
            bytes_accessed=2 * (depth * columns + rows * columns),
            transcendentals=0,
        ),
    )(head_latent, w_absorb_v, w_out)


def dispatch_kernel(partial_ref, gain_ref, place_ref, out_ref, wide):
    devs, requests, width = partial_ref.shape
    tile = width // 8
    square = jnp.zeros((requests, 1), F32)
    for t in range(0, width, tile):
        total = partial_ref[0, :, t : t + tile].astype(F32)
        for d in range(1, devs):
            total += partial_ref[d, :, t : t + tile].astype(F32)
        attended = total.astype(BF16).astype(F32)
        wide[:, t : t + tile] = attended
        square += jnp.sum(attended * attended, axis=1, keepdims=True)
    factor = lax.rsqrt(square / width + 1e-06)
    for t in range(0, width, tile):
        normed = (wide[:, t : t + tile] * factor * gain_ref[:, t : t + tile]).astype(BF16)
        rows = jnp.dot(place_ref[...], normed, preferred_element_type=F32).astype(BF16)
        for e in range(out_ref.shape[0]):
            out_ref[e, :, t : t + tile] = rows[e * CAP : (e + 1) * CAP]


def dispatch_rows(partial, gain, place):
    _, requests, width = partial.shape
    slots = place.shape[0]
    return pl.pallas_call(
        dispatch_kernel,
        out_shape=jax.ShapeDtypeStruct((slots // CAP, CAP, width), BF16),
        in_specs=[pl.BlockSpec(memory_space=pltpu.VMEM)] * 3,
        out_specs=pl.BlockSpec(memory_space=pltpu.VMEM),
        scratch_shapes=[pltpu.VMEM((requests, width), F32)],
        compiler_params=pltpu.CompilerParams(vmem_limit_bytes=10 * 1024 * 1024),
        cost_estimate=pl.CostEstimate(
            flops=2 * slots * requests * width,
            bytes_accessed=2 * partial.size,
            transcendentals=0,
        ),
    )(partial, gain, place)


def mix_kernel(ring, weight_ref, rows_ref, out_ref):
    width = rows_ref.shape[2]
    slots = weight_ref.shape[1]
    experts = slots // CAP
    shards = rows_ref.shape[0] // experts
    for z in range(ring):
        rows = jnp.concatenate(
            [
                sum(rows_ref[e * shards + s].astype(F32) for s in range(z, shards, ring))
                for e in range(experts)
            ],
            axis=0,
        )
        out_ref[:, z * width : (z + 1) * width] = jnp.dot(
            weight_ref[...], rows, precision=lax.Precision.HIGHEST, preferred_element_type=F32
        ).astype(BF16)


def mix(weight, rows, ring):
    requests, slots = weight.shape
    width = rows.shape[2]
    return pl.pallas_call(
        functools.partial(mix_kernel, ring),
        out_shape=jax.ShapeDtypeStruct((requests, ring * width), BF16),
        in_specs=[pl.BlockSpec(memory_space=pltpu.VMEM)] * 2,
        out_specs=pl.BlockSpec(memory_space=pltpu.VMEM),
        compiler_params=pltpu.CompilerParams(vmem_limit_bytes=10 * 1024 * 1024),
        cost_estimate=pl.CostEstimate(
            flops=2 * requests * slots * ring * width,
            bytes_accessed=2 * rows.size,
            transcendentals=0,
        ),
    )(weight, rows)


def per_device(
    q_nope,
    q_rope,
    w_absorb_k,
    latent_cache,
    rope_keys,
    cache_lengths,
    w_absorb_v,
    w_out,
    norm_gain,
    routes,
    expert_probs,
    group_probs,
    w_gate,
    w_up,
    w_down,
):
    batch_rows = q_nope.shape[0]
    heads_local, nope_width, latent_width = w_absorb_k.shape
    rope_width = q_rope.shape[1] // heads_local
    model_width = w_out.shape[1]
    requests, _, cache_len = rope_keys.shape
    devs = lax.axis_size("dev")
    groups = lax.axis_size("grp")
    shards = devs // EXP_GRP
    experts = EXP_GRP * groups
    top_count = routes.shape[1]
    softmax_scale = float(nope_width + rope_width) ** (-0.5)

    ring = shards // 2
    z_up = [(i, i // ring * ring + (i + 1) % ring) for i in range(devs)]
    z_down = [(i, i // ring * ring + (i + ring - 1) % ring) for i in range(devs)]
    y_pair = [(i, i ^ ring) for i in range(devs)]

    units = w_down.shape[1]
    place = lax.axis_index("dev") % shards
    split = shards // ring
    half_width = model_width // shards
    layout = [(0, 0), (1, 0), (3, 0), (2, 0)]
    widths = [half_width * split] * ring
    down_out = column_blocks(w_down, layout, ring, widths)

    def relay(i):
        way = [(j, j // ring * ring + (j + layout[i][0]) % ring) for j in range(devs)]
        return lax.ppermute(down_out[i], "dev", way)

    query = absorb(q_nope, q_rope, w_absorb_k)
    query = query.reshape(devs, requests, query.shape[1])
    query = lax.all_to_all(query, "dev", split_axis=0, concat_axis=0, tiled=True)
    down = [down_out[0], relay(1), relay(2)]
    latent_out, w_out = attend(
        query, latent_cache, rope_keys, cache_lengths, w_out, heads_local, softmax_scale
    )
    head_latent = lax.all_to_all(latent_out, "dev", split_axis=0, concat_axis=0, tiled=True)
    partial = project(
        head_latent.reshape(batch_rows, heads_local * latent_width), w_absorb_v, w_out
    )
    partial, down, down_out = lax.optimization_barrier((partial, down, down_out))
    partial = lax.all_to_all(
        partial.reshape(devs, requests, model_width),
        "dev",
        split_axis=0,
        concat_axis=0,
        tiled=True,
    )
    flat_routes = routes.reshape(requests * top_count)
    chosen = (flat_routes[:, None] == jnp.arange(experts)[None, :]).astype(jnp.int32)
    earlier = jnp.cumsum(chosen, axis=0) - chosen
    rank_in = jnp.sum(earlier * chosen, axis=1)
    slot_index = (flat_routes * CAP + rank_in).reshape(requests, top_count)
    slot_ids = jnp.arange(experts * CAP)
    placed = slot_index[None, :, :] == slot_ids[:, None, None]
    dispatch = jnp.any(placed, axis=2).astype(BF16)
    group_match = (routes // EXP_GRP)[:, :, None] == jnp.arange(groups)[None, None, :]
    group_weight = jnp.sum(jnp.where(group_match, group_probs[:, None, :], 0.0), axis=2)
    pair_weight = group_weight * expert_probs
    slot_weight = jnp.sum(jnp.where(placed, pair_weight[None], 0.0), axis=2).T

    partial, down_out, dispatch, slot_weight = lax.optimization_barrier(
        (partial, down_out, dispatch, slot_weight)
    )
    down = [*down, relay(3)]

    outgoing = dispatch_rows(partial, norm_gain[None, :], dispatch)

    peers = [
        [g * devs + half * shards + p for g in range(groups) for half in range(EXP_GRP)]
        for p in range(shards)
    ]
    own = lax.all_to_all(
        outgoing,
        ("grp", "dev"),
        split_axis=0,
        concat_axis=0,
        tiled=True,
        axis_index_groups=peers,
    ).reshape(experts * CAP, model_width)

    own, down = lax.optimization_barrier((own, down))

    half_rows = own.shape[0] // 2
    lo, hi = slice(0, half_rows), slice(half_rows, None)

    def send(value, way):
        return lax.ppermute(value, "dev", way)

    below_lo = send(own[lo], z_up)
    above_hi = send(own[hi], z_down)
    beside = send(own, y_pair)
    below_hi = send(own[hi], z_up)
    above_lo = send(own[lo], z_down)
    first = expert_hidden([own, below_lo, below_hi, above_lo, above_hi, beside], w_gate, w_up)
    far_lo = send(below_lo, z_up)
    far_hi = send(above_hi, z_down)
    beside_below_lo = send(beside[lo], z_up)
    beside_above_hi = send(beside[hi], z_down)
    beside_below_hi = send(below_hi, y_pair)
    above_lo, beside_below_hi = lax.optimization_barrier((above_lo, beside_below_hi))
    beside_above_lo = send(above_lo, y_pair)
    second = expert_hidden(
        [far_lo, far_hi, beside_below_lo, beside_below_hi, beside_above_lo, beside_above_hi],
        w_gate,
        w_up,
    )
    beside_far_lo = send(beside_below_lo, z_up)
    beside_far_hi = send(beside_above_hi, z_down)
    beside_far_lo, beside_far_hi, first, second = lax.optimization_barrier(
        (beside_far_lo, beside_far_hi, first, second)
    )
    third = expert_hidden([beside_far_lo, beside_far_hi], w_gate, w_up)
    rows = own.shape[0]
    relative = jnp.concatenate([first, second, third], axis=0).reshape(shards, rows, units)
    order = jnp.array([0, 1, 4, 2, 3, 5, 7, 6], jnp.int32)
    position = jnp.arange(shards, dtype=jnp.int32)
    other = (position // ring) ^ (place // ring)
    steps = (place % ring - position % ring) % ring
    hidden = relative[order[other * ring + steps]].reshape(shards * rows, units)
    everyone = jnp.broadcast_to(hidden[None], (ring, shards * rows, units))
    rings = [[start + z for z in range(ring)] for start in range(0, devs, ring)]
    everyone = lax.all_to_all(
        everyone, "dev", split_axis=0, concat_axis=0, tiled=True, axis_index_groups=rings
    )
    result = expert_down(everyone, down, layout, groups, split)
    result = lax.all_to_all(result, ("grp", "dev"), split_axis=0, concat_axis=0, tiled=True)
    return mix(slot_weight, result, ring)


def solution(mesh):
    placed = (
        P("grp", "dev"),
        P("grp", "dev"),
        P("dev", None, None),
        P(("grp", "dev"), None, None),
        P(("grp", "dev"), None, None),
        P(("grp", "dev")),
        P("dev", None, None),
        P("dev", None),
        P(),
        P(("grp", "dev"), None),
        P(("grp", "dev"), None),
        P(("grp", "dev"), None),
        P(("grp", "dev"), None, None),
        P(("grp", "dev"), None, None),
        P(("grp", "dev"), None, None),
    )
    return jax.shard_map(
        per_device, mesh=mesh, in_specs=placed, out_specs=P(("grp", "dev"), None), check_vma=False
    )
```
